32 devices in a mesh: rows: 8 (over y, x, core), grp: 4 (over z).
Axes of the slice: x: 2, y: 2, z: 4, core: 2. Of those that a mesh axis runs over, the one named last changes fastest.
Arguments:
- hc_edge: bfloat16 [65536, 512], P(('rows', 'grp')), may hold values from -6 to 6
- hp_edge: bfloat16 [65536, 512], P(('rows', 'grp')), may hold values from -6 to 6
- cust_count: int32 [32, 32], P(('rows', 'grp')), may hold values from 0 to 64, as said below
- recv_key: int32 [65536], P(('rows', 'grp')), may hold values from 0 to 2047
- prod_key: int32 [65536], P(('rows', 'grp')), may hold values from 0 to 255
- cust_grad: bfloat16 [65536, 512], P(('rows', 'grp')), may hold values from -6 to 6
- prod_grad: bfloat16 [256, 512], P(('rows', 'grp')), may hold values from -6 to 6
- w_cust: bfloat16 [512, 512], replicated, may hold values from -0.25 to 0.25
- w_prod: bfloat16 [512, 512], replicated, may hold values from -0.25 to 0.25
Outputs:
- cust_table_grad: float32 [65536, 512], P(('rows', 'grp'))
- prod_table_grad: float32 [256, 512], P(('rows', 'grp'))
- w_cust_grad: float32 [512, 512], replicated
- w_prod_grad: float32 [512, 512], replicated
The draws below stay inside these ranges and needn't reach their ends.
Inputs may be any that keep to these rules, and one draw needn't show every extreme that they name: `cust_count`: entry [i, j] counts the live slots of device i's block for owner j; every device fills its block to 64 for one or more owners, which differ between draws. `recv_key`: keys of slots past a block's count are ignored. `prod_key`: ids of slots that are not live are ignored.
All inputs are finite; a program needn't handle non-finite values.
Results may differ from the reference program's by a relative error of at most 0.0034.
Values may be sent and summed in bfloat16 or wider, within the bound.
No kernel may reach another device: no remote copies, remote signals or barrier semaphores. Data moves between devices by JAX's collectives and lax.ppermute only.
A program may use at most 64 MiB of HBM per device.

```python
import math
import jax
import jax.numpy as jnp
import numpy as np
from jax import lax

D = 512
E_DEV = 2048
C_DEV = 2048
P_DEV = 8
CAP = 64
SLOTS = 65536
CUSTOMERS = 65536
PRODUCTS = 256
N_ROWS = 8
N_GRP = 4


def draw_cust_count(key, part):
    devices = N_ROWS * N_GRP
    first_key = jax.random.fold_in(key, 11)
    second_key = jax.random.fold_in(key, 23)
    third_key = jax.random.fold_in(key, 37)
    hot_owner = jax.random.randint(first_key, (devices,), 0, 8) == 0
    forced_owner = jax.random.randint(second_key, (), 0, devices)
    hot_owner = hot_owner | (jnp.arange(devices, dtype=jnp.int32) == forced_owner)
    base_counts = jax.random.randint(third_key, (devices, devices), CAP // 4, CAP // 2 + 1)
    return jnp.where(hot_owner[None, :], CAP, base_counts).astype(jnp.int32)


def place_ends(entries, own_key, low, top_value):
    longest = entries.shape.index(max(entries.shape))
    spots = []
    for shift in (0, 1):
        where = [jax.random.randint(jax.random.fold_in(own_key, axis), (), 0, length) for axis, length in enumerate(entries.shape)]
        where[longest] = (where[longest] + shift) % entries.shape[longest]
        spots.append(tuple(where))
    return entries.at[spots[0]].set(low).at[spots[1]].set(top_value)


def levels(rng, extent, shards, least, high):
    loudness, own = 1.0, jax.random.fold_in(rng, 6)
    for axis_at, blocks in shards:
        draws = jnp.exp(jax.random.uniform(jax.random.fold_in(own, axis_at), (blocks,), jnp.float32, least / len(shards), high / len(shards)))
        loudness = loudness * jnp.repeat(draws, extent[axis_at] // blocks).reshape([-1 if axis == axis_at else 1 for axis in range(len(extent))])
    return loudness


def rank_bounds(number_of, skew):
    loads = [(1 << 20) // math.isqrt(standing ** skew) + 1 for standing in range(1, number_of + 1)]
    deviation = 1 + sum(loads) // (1 << 30)
    return np.cumsum(np.array([max(1, weight // deviation) for weight in loads]))


def ranked_ids(key, dims, number_of, skew):
    table = rank_bounds(number_of, skew)
    ticket = jax.random.randint(jax.random.fold_in(key, 1), dims, 0, int(table[number_of - 1]))
    grade = jnp.searchsorted(jnp.asarray(table, jnp.int32), ticket, side="right")
    return jax.random.permutation(jax.random.fold_in(key, 2), number_of)[grade].astype(jnp.int32)


def bell_draw(stream_key, dims, deviation, limit, cuts=(), held_as=jnp.bfloat16):
    entries = deviation * jax.random.normal(stream_key, dims, jnp.float32)
    if cuts:
        entries = entries * levels(stream_key, dims, cuts, -0.22, 0.18)
    return jnp.clip(entries, -limit, limit).astype(held_as)


def setup_inputs(seed: int = 0) -> dict:
    key_of = jax.random.split(jax.random.key(seed), 10)
    hc_edge = bell_draw(key_of[0], (SLOTS, D), 1.0, 6.0, ((0, 32),))
    hp_edge = bell_draw(key_of[1], (SLOTS, D), 1.0, 6.0, ((0, 32),))
    cust_count = draw_cust_count(jax.random.fold_in(key_of[9], 71), 0)
    recv_key = place_ends(jax.random.randint(key_of[3], (SLOTS,), 0, C_DEV), jax.random.fold_in(key_of[3], 1), 0, C_DEV - 1).astype(jnp.int32)
    prod_key = place_ends(ranked_ids(key_of[4], (SLOTS,), PRODUCTS, 1), jax.random.fold_in(key_of[4], 3), 0, PRODUCTS - 1).astype(jnp.int32)
    cust_grad = bell_draw(key_of[5], (CUSTOMERS, D), 1.0, 6.0, ((0, 32),))
    prod_grad = bell_draw(key_of[6], (PRODUCTS, D), 1.0, 6.0, ((0, 32),))
    w_cust = bell_draw(key_of[7], (D, D), D ** -0.5, 0.25)
    w_prod = bell_draw(key_of[8], (D, D), D ** -0.5, 0.25)
    return {"hc_edge": hc_edge, "hp_edge": hp_edge, "cust_count": cust_count, "recv_key": recv_key, "prod_key": prod_key, "cust_grad": cust_grad, "prod_grad": prod_grad, "w_cust": w_cust, "w_prod": w_prod}


def reference(hc_edge, hp_edge, cust_count, recv_key, prod_key, cust_grad, prod_grad, w_cust, w_prod):
    devices = N_ROWS * N_GRP
    owner_keys = recv_key.reshape(devices, devices, CAP)
    owner_base = (jnp.arange(devices, dtype=jnp.int32) * C_DEV)[None, :, None]
    cust_ids = (jnp.transpose(owner_keys, (1, 0, 2)) + owner_base).astype(jnp.int32)
    live_mask = jnp.arange(CAP, dtype=jnp.int32)[None, None, :] < cust_count[:, :, None]
    hc_blocks = hc_edge.reshape(devices, E_DEV, D)
    hp_blocks = hp_edge.reshape(devices, E_DEV, D)
    id_blocks = cust_ids.reshape(devices, E_DEV)
    live_blocks = live_mask.reshape(devices, E_DEV)
    prod_blocks = prod_key.reshape(devices, E_DEV)

    def per_source(carry, inputs):
        cust_acc, prod_acc, wc_acc, wp_acc = carry
        hc_block, hp_block, id_block, live_block, prod_block = inputs
        preact = jnp.dot(hc_block, w_cust, preferred_element_type=jnp.float32) + jnp.dot(hp_block, w_prod, preferred_element_type=jnp.float32)
        squashed = jax.nn.sigmoid(preact)
        fetched = jnp.take(cust_grad, id_block, axis=0).astype(jnp.float32) + jnp.take(prod_grad, prod_block, axis=0).astype(jnp.float32)
        upstream = jnp.where(live_block[:, None], fetched, jnp.float32(0.0))
        delta = (upstream * squashed * (1.0 + preact * (1.0 - squashed))).astype(jnp.bfloat16)
        delta_wide = delta.astype(jnp.float32)
        cust_acc = cust_acc.at[id_block].add(delta_wide)
        prod_acc = prod_acc.at[prod_block].add(delta_wide)
        wc_acc = wc_acc + jnp.dot(hc_block.T, delta, preferred_element_type=jnp.float32)
        wp_acc = wp_acc + jnp.dot(hp_block.T, delta, preferred_element_type=jnp.float32)
        return ((cust_acc, prod_acc, wc_acc, wp_acc), None)
    start_carry = (jnp.zeros((CUSTOMERS, D), jnp.float32), jnp.zeros((PRODUCTS, D), jnp.float32), jnp.zeros((D, D), jnp.float32), jnp.zeros((D, D), jnp.float32))
    final_carry, unused = lax.scan(per_source, start_carry, (hc_blocks, hp_blocks, id_blocks, live_blocks, prod_blocks))
    cust_acc, prod_acc, wc_acc, wp_acc = final_carry
    cust_sum = cust_acc.astype(jnp.bfloat16)
    prod_sum = prod_acc.astype(jnp.bfloat16)
    cust_table_grad = jnp.dot(cust_sum, w_cust.T, preferred_element_type=jnp.float32)
    prod_table_grad = jnp.dot(prod_sum, w_prod.T, preferred_element_type=jnp.float32) * math.sqrt(P_DEV / E_DEV)
    grad_scale = 1.0 / math.sqrt(E_DEV * devices)
    return (cust_table_grad, prod_table_grad, wc_acc * grad_scale, wp_acc * grad_scale)
```

```python
import math

import jax
import jax.numpy as jnp
from jax import lax
from jax.sharding import PartitionSpec as P

AXES = ("rows", "grp")


def shift_rows(value, mask):
    size = lax.axis_size("rows")
    return lax.ppermute(value, "rows", [(i, i ^ mask) for i in range(size)])


def shift_grp(value, mask):
    size = lax.axis_size("grp")
    return lax.ppermute(value, "grp", [(i, i ^ mask) for i in range(size)])


def place():
    row = lax.axis_index("rows")
    return row % 2, row // 2, lax.axis_index("grp")


def spread(mine, shift, size, step, here):
    blocks = [mine] + [shift(mine, step * k) for k in range(1, size)]
    stacked = jnp.zeros((size,) + mine.shape, mine.dtype)
    for k, block in enumerate(blocks):
        stacked = lax.dynamic_update_index_in_dim(stacked, block, here ^ k, 0)
    return stacked


def gather_all(mine):
    core, plane, grp = place()
    planes = lax.axis_size("rows") // 2
    own = spread(mine, shift_grp, lax.axis_size("grp"), 1, grp)
    own = spread(own, shift_rows, planes, 2, plane)
    other = shift_rows(own, 1)
    first = core == 0
    return jnp.stack([jnp.where(first, own, other), jnp.where(first, other, own)])


def fold(terms, shift, size, step, here):
    total = lax.dynamic_index_in_dim(terms, here, 0, False)
    leaving = terms.astype(jnp.bfloat16)
    for k in range(1, size):
        sent = lax.dynamic_index_in_dim(leaving, here ^ k, 0, False)
        total = total + shift(sent, step * k).astype(jnp.float32)
    return total


def reduce_all(terms):
    core, plane, grp = place()
    sent = lax.dynamic_index_in_dim(terms, 1 - core, 0, False)
    kept = lax.dynamic_index_in_dim(terms, core, 0, False) + shift_rows(sent, 1)
    kept = fold(kept, shift_rows, lax.axis_size("rows") // 2, 2, plane)
    return fold(kept, shift_grp, lax.axis_size("grp"), 1, grp)


def body(hc_edge, hp_edge, cust_count, recv_key, prod_key, cust_grad, prod_grad, w_cust, w_prod):
    devices = lax.axis_size(AXES)
    grps = lax.axis_size("grp")
    planes = lax.axis_size("rows") // 2
    slot_count, width = hc_edge.shape
    capacity = slot_count // devices
    product_count = prod_grad.shape[0]
    grid = (2, planes, grps)

    owned_rows = jnp.take(cust_grad, recv_key, axis=0, mode="clip")
    fetched = lax.all_to_all(
        owned_rows.reshape(devices, capacity, width), AXES, split_axis=0, concat_axis=0, tiled=True
    ).reshape(slot_count, width)

    owner, low = prod_key // product_count, prod_key % product_count
    row, grp = owner // grps, owner % grps
    prod_at = (((row % 2) * planes + row // 2) * grps + grp) * product_count + low
    product_table = gather_all(prod_grad).reshape(devices * product_count, width)
    product_rows = jnp.take(product_table, prod_at, axis=0, mode="clip")

    preact = jnp.dot(hc_edge, w_cust, preferred_element_type=jnp.float32) + jnp.dot(
        hp_edge, w_prod, preferred_element_type=jnp.float32
    )
    squashed = jax.nn.sigmoid(preact)
    live_mask = (
        jnp.arange(capacity, dtype=jnp.int32)[None, :] < cust_count.reshape(devices, 1)
    ).reshape(slot_count)
    gate = jnp.where(live_mask[:, None], squashed * (1.0 + preact * (1.0 - squashed)), 0.0)
    gate, product_rows = lax.optimization_barrier((gate, product_rows))

    upstream = fetched.astype(jnp.float32) + product_rows.astype(jnp.float32)
    delta = (upstream * gate).astype(jnp.bfloat16)

    returned = lax.all_to_all(
        delta.reshape(devices, capacity, width), AXES, split_axis=0, concat_axis=0, tiled=True
    ).reshape(slot_count, width)

    wanted = jnp.arange(devices * product_count, dtype=jnp.int32)
    product_hot = (prod_at[None, :] == wanted[:, None]).astype(jnp.bfloat16)
    contract = (((0,), (0,)), ((), ()))
    terms = jnp.concatenate(
        [
            jnp.dot(product_hot, delta, preferred_element_type=jnp.float32).reshape(*grid, -1, width),
            lax.dot_general(
                hc_edge, delta, contract, preferred_element_type=jnp.float32
            ).reshape(*grid, -1, width),
            lax.dot_general(
                hp_edge, delta, contract, preferred_element_type=jnp.float32
            ).reshape(*grid, -1, width),
        ],
        axis=3,
    )
    mine = reduce_all(terms)
    prod_table_grad = lax.dot_general(
        mine[:product_count],
        w_prod.astype(jnp.float32),
        (((1,), (1,)), ((), ())),
        precision=lax.Precision.HIGHEST,
        preferred_element_type=jnp.float32,
    ) * math.sqrt(product_count / slot_count)
    grad_scale = 1.0 / math.sqrt(slot_count * devices)
    share = width // devices
    weights = gather_all(mine[product_count:].astype(jnp.bfloat16)).astype(jnp.float32) * grad_scale
    cust_weight = weights[..., :share, :].reshape(width, width)
    prod_weight = weights[..., share:, :].reshape(width, width)

    owned_count = cust_grad.shape[0]
    one_hot = (recv_key[None, :] == jnp.arange(owned_count, dtype=jnp.int32)[:, None]).astype(
        jnp.bfloat16
    )
    cust_sum = jnp.dot(one_hot, returned, preferred_element_type=jnp.float32).astype(jnp.bfloat16)
    cust_table_grad = lax.dot_general(
        cust_sum, w_cust, (((1,), (1,)), ((), ())), preferred_element_type=jnp.float32
    )
    return cust_table_grad, prod_table_grad, cust_weight, prod_weight


def solution(mesh):
    rows = P(AXES, None)
    placed = (rows, rows, rows, P(AXES), P(AXES), rows, rows, P(), P())
    return jax.shard_map(
        body,
        mesh=mesh,
        in_specs=placed,
        out_specs=(rows, rows, P(), P()),
        check_vma=False,
    )
```

```python
import math

import jax
import jax.numpy as jnp
from jax import lax
from jax.experimental import pallas as pl
from jax.experimental.pallas import tpu as pltpu
from jax.sharding import PartitionSpec as P

AXES = ("rows", "grp")


def shift_rows(value, mask):
    size = lax.axis_size("rows")
    return lax.ppermute(value, "rows", [(i, i ^ mask) for i in range(size)])


def shift_grp(value, mask):
    size = lax.axis_size("grp")
    return lax.ppermute(value, "grp", [(i, i ^ mask) for i in range(size)])


def pick_kernel(key_ref, table_ref, out_ref):
    tile, length = key_ref.shape[1], table_ref.shape[0]
    keys = jnp.transpose(jnp.broadcast_to(key_ref[...], (128, tile)))
    lane = lax.broadcasted_iota(jnp.int32, (tile, 128), 1)
    one, zero = jnp.bfloat16(1), jnp.bfloat16(0)
    hot = jnp.concatenate(
        [jnp.where(keys == lane + at, one, zero) for at in range(0, length, 128)], axis=1
    )
    out_ref[...] = jnp.dot(hot, table_ref[...], preferred_element_type=jnp.float32).astype(
        jnp.bfloat16
    )


def pick(table, keys, tile=512):
    length, width = table.shape
    count = keys.shape[0]
    tile = min(tile, count)
    return pl.pallas_call(
        pick_kernel,
        grid=(count // tile,),
        out_shape=jax.ShapeDtypeStruct((count, width), jnp.bfloat16),
        in_specs=[
            pl.BlockSpec((1, tile), lambda i: (0, i)),
            pl.BlockSpec((length, width), lambda i: (0, 0)),
        ],
        out_specs=pl.BlockSpec((tile, width), lambda i: (i, 0)),
        compiler_params=pltpu.CompilerParams(vmem_limit_bytes=32 << 20),
        cost_estimate=pl.CostEstimate(
            flops=2 * count * length * width,
            bytes_accessed=2 * (length + count) * width,
            transcendentals=0,
        ),
        name="pick_rows",
    )(keys.reshape(1, count), table)


def place():
    row = lax.axis_index("rows")
    return row % 2, row // 2, lax.axis_index("grp")


def spread(mine, shift, size, step, here):
    blocks = [mine] + [shift(mine, step * k) for k in range(1, size)]
    stacked = jnp.zeros((size,) + mine.shape, mine.dtype)
    for k, block in enumerate(blocks):
        stacked = lax.dynamic_update_index_in_dim(stacked, block, here ^ k, 0)
    return stacked


def gather_grp(mine):
    return spread(mine, shift_grp, lax.axis_size("grp"), 1, lax.axis_index("grp"))


def gather_rows(own):
    core, plane, grp = place()
    own = spread(own, shift_rows, lax.axis_size("rows") // 2, 2, plane)
    other = shift_rows(own, 1)
    first = core == 0
    return jnp.stack([jnp.where(first, own, other), jnp.where(first, other, own)])


def fold(terms, shift, size, step, here):
    total = lax.dynamic_index_in_dim(terms, here, 0, False)
    leaving = terms.astype(jnp.bfloat16)
    for k in range(1, size):
        sent = lax.dynamic_index_in_dim(leaving, here ^ k, 0, False)
        total = total + shift(sent, step * k).astype(jnp.float32)
    return total


def reduce_all(terms):
    core, plane, grp = place()
    sent = lax.dynamic_index_in_dim(terms, 1 - core, 0, False)
    kept = lax.dynamic_index_in_dim(terms, core, 0, False) + shift_rows(sent, 1)
    kept = fold(kept, shift_rows, lax.axis_size("rows") // 2, 2, plane)
    return fold(kept, shift_grp, lax.axis_size("grp"), 1, grp)


def body(hc_edge, hp_edge, cust_count, recv_key, prod_key, cust_grad, prod_grad, w_cust, w_prod):
    devices = lax.axis_size(AXES)
    grps = lax.axis_size("grp")
    planes = lax.axis_size("rows") // 2
    slot_count, width = hc_edge.shape
    capacity = slot_count // devices
    product_count = prod_grad.shape[0]
    grid = (2, planes, grps)

    products = gather_grp(prod_grad)
    owned_rows = pick(cust_grad, recv_key)
    owned_rows, products = lax.optimization_barrier((owned_rows, products))
    fetched = lax.all_to_all(
        owned_rows.reshape(devices, capacity, width), AXES, split_axis=0, concat_axis=0, tiled=True
    ).reshape(slot_count, width)

    owner, low = prod_key // product_count, prod_key % product_count
    row, grp = owner // grps, owner % grps
    prod_at = (((row % 2) * planes + row // 2) * grps + grp) * product_count + low
    product_table = gather_rows(products).reshape(devices * product_count, width)
    product_rows = pick(product_table, prod_at)

    preact = jnp.dot(hc_edge, w_cust, preferred_element_type=jnp.float32) + jnp.dot(
        hp_edge, w_prod, preferred_element_type=jnp.float32
    )
    squashed = jax.nn.sigmoid(preact)
    live_mask = (
        jnp.arange(capacity, dtype=jnp.int32)[None, :] < cust_count.reshape(devices, 1)
    ).reshape(slot_count)
    gate = jnp.where(live_mask[:, None], squashed * (1.0 + preact * (1.0 - squashed)), 0.0)
    gate, product_rows = lax.optimization_barrier((gate, product_rows))

    upstream = fetched.astype(jnp.float32) + product_rows.astype(jnp.float32)
    delta = (upstream * gate).astype(jnp.bfloat16)

    returned = lax.all_to_all(
        delta.reshape(devices, capacity, width), AXES, split_axis=0, concat_axis=0, tiled=True
    ).reshape(slot_count, width)

    edge = shift_rows(delta[:16], 1)
    delta, edge = lax.optimization_barrier((delta, edge))
    wanted = jnp.arange(devices * product_count, dtype=jnp.int32)
    product_hot = (prod_at[None, :] == wanted[:, None]).astype(jnp.bfloat16)
    contract = (((0,), (0,)), ((), ()))
    terms = jnp.concatenate(
        [
            jnp.dot(product_hot, delta, preferred_element_type=jnp.float32).reshape(*grid, -1, width),
            lax.dot_general(
                hc_edge, delta, contract, preferred_element_type=jnp.float32
            ).reshape(*grid, -1, width),
            lax.dot_general(
                hp_edge, delta, contract, preferred_element_type=jnp.float32
            ).reshape(*grid, -1, width),
        ],
        axis=3,
    )
    mine = reduce_all(terms)
    mine, returned = lax.optimization_barrier((mine, returned))
    prod_table_grad = lax.dot_general(
        mine[:product_count],
        w_prod.astype(jnp.float32),
        (((1,), (1,)), ((), ())),
        precision=lax.Precision.HIGHEST,
        preferred_element_type=jnp.float32,
    ) * math.sqrt(product_count / slot_count)
    grad_scale = 1.0 / math.sqrt(slot_count * devices)
    share = width // devices
    own = gather_grp(mine[product_count:].astype(jnp.bfloat16))
    wanted = jnp.arange(cust_grad.shape[0], dtype=jnp.int32)
    one_hot = (recv_key[None, :] == wanted[:, None]).astype(jnp.bfloat16)
    cust_sum = jnp.dot(one_hot, returned, preferred_element_type=jnp.float32).astype(jnp.bfloat16)
    own, cust_sum = lax.optimization_barrier((own, cust_sum))
    own = spread(own, shift_rows, planes, 2, lax.axis_index("rows") // 2)
    cust_table_grad = lax.dot_general(
        cust_sum, w_cust, (((1,), (1,)), ((), ())), preferred_element_type=jnp.float32
    )
    own, prod_table_grad, cust_table_grad = lax.optimization_barrier(
        (own, prod_table_grad, cust_table_grad)
    )
    other = shift_rows(own, 1)

    def whole(share_at):
        pick_share = slice(share_at, share_at + share)
        mine_part, other_part = own[:, :, pick_share], other[:, :, pick_share]
        first = lax.axis_index("rows") % 2 == 0
        both = [jnp.where(first, mine_part, other_part), jnp.where(first, other_part, mine_part)]
        return jnp.stack(both).astype(jnp.float32).reshape(width, width) * grad_scale

    return cust_table_grad, prod_table_grad, whole(0), whole(share)


def solution(mesh):
    rows = P(AXES, None)
    placed = (rows, rows, rows, P(AXES), P(AXES), rows, rows, P(), P())
    return jax.shard_map(
        body,
        mesh=mesh,
        in_specs=placed,
        out_specs=(rows, rows, P(), P()),
        check_vma=False,
    )
```

```python
import functools
import math

import jax
import jax.numpy as jnp
from jax import lax
from jax.experimental import pallas as pl
from jax.experimental.pallas import tpu as pltpu
from jax.sharding import PartitionSpec as P

AXES = ("rows", "grp")


def shift_rows(value, mask):
    size = lax.axis_size("rows")
    return lax.ppermute(value, "rows", [(i, i ^ mask) for i in range(size)])


def shift_grp(value, mask):
    size = lax.axis_size("grp")
    return lax.ppermute(value, "grp", [(i, i ^ mask) for i in range(size)])


def pick_kernel(key_ref, table_ref, out_ref):
    tile, length = key_ref.shape[1], table_ref.shape[0]
    keys = jnp.transpose(jnp.broadcast_to(key_ref[...], (128, tile)))
    lane = lax.broadcasted_iota(jnp.int32, (tile, 128), 1)
    one, zero = jnp.bfloat16(1), jnp.bfloat16(0)
    hot = jnp.concatenate(
        [jnp.where(keys == lane + at, one, zero) for at in range(0, length, 128)], axis=1
    )
    out_ref[...] = jnp.dot(hot, table_ref[...], preferred_element_type=jnp.float32).astype(
        jnp.bfloat16
    )


def pick(table, keys, space, limit, tile=512):
    length, width = table.shape
    count = keys.shape[0]
    tile = min(tile, count)
    return pl.pallas_call(
        pick_kernel,
        grid=(count // tile,),
        out_shape=space((count, width), jnp.bfloat16),
        in_specs=[
            pl.BlockSpec((1, tile), lambda i: (0, i)),
            pl.BlockSpec((length, width), lambda i: (0, 0)),
        ],
        out_specs=pl.BlockSpec((tile, width), lambda i: (i, 0)),
        compiler_params=pltpu.CompilerParams(vmem_limit_bytes=limit << 20),
        cost_estimate=pl.CostEstimate(
            flops=2 * count * length * width,
            bytes_accessed=2 * (length + count) * width,
            transcendentals=0,
        ),
        name="pick_rows",
    )(keys.reshape(1, count), table)


def gate_kernel(count_ref, hc_ref, hp_ref, wc_ref, wp_ref, out_ref, *, capacity):
    blocks = out_ref.shape[0] // capacity
    preact = jnp.dot(hc_ref[...], wc_ref[...], preferred_element_type=jnp.float32) + jnp.dot(
        hp_ref[...], wp_ref[...], preferred_element_type=jnp.float32
    )
    squashed = jax.nn.sigmoid(preact)
    slot = lax.broadcasted_iota(jnp.int32, (capacity, 1), 0)
    first = pl.program_id(0) * blocks
    live = jnp.concatenate([slot < count_ref[0, first + k] for k in range(blocks)])
    out_ref[...] = jnp.where(live, squashed * (1.0 + preact * (1.0 - squashed)), 0.0)


def slot_gate(cust_count, hc_edge, hp_edge, w_cust, w_prod, tile=512):
    count, width = hc_edge.shape
    tile = min(tile, count)
    slots = pl.BlockSpec((tile, width), lambda i, c: (i, 0))
    whole = pl.BlockSpec((width, width), lambda i, c: (0, 0))
    return pl.pallas_call(
        functools.partial(gate_kernel, capacity=count // cust_count.shape[1]),
        grid_spec=pltpu.PrefetchScalarGridSpec(
            num_scalar_prefetch=1,
            grid=(count // tile,),
            in_specs=[slots, slots, whole, whole],
            out_specs=slots,
        ),
        out_shape=pltpu.VMEM((count, width), jnp.float32),
        compiler_params=pltpu.CompilerParams(vmem_limit_bytes=32 << 20),
        cost_estimate=pl.CostEstimate(
            flops=4 * count * width * width,
            bytes_accessed=8 * count * width,
            transcendentals=count * width,
        ),
        name="slot_gate",
    )(cust_count, hc_edge, hp_edge, w_cust, w_prod)


def terms_kernel(half_ref, at_ref, hc_ref, hp_ref, delta_ref, out_ref):
    delta = delta_ref[...]
    columns = hc_ref.shape[1]
    products = out_ref.shape[0] - 2 * columns
    wanted = half_ref[0] * products + lax.broadcasted_iota(jnp.int32, (products, 1), 0)
    hot = jnp.where(at_ref[...] == wanted, jnp.bfloat16(1), jnp.bfloat16(0))
    contract = (((0,), (0,)), ((), ()))
    parts = (
        jnp.dot(hot, delta, preferred_element_type=jnp.float32),
        lax.dot_general(hc_ref[...], delta, contract, preferred_element_type=jnp.float32),
        lax.dot_general(hp_ref[...], delta, contract, preferred_element_type=jnp.float32),
    )
    starts = (0, products, products + columns)

    @pl.when(pl.program_id(0) == 0)
    def _():
        for at, part in zip(starts, parts):
            out_ref[at : at + part.shape[0], :] = part

    @pl.when(pl.program_id(0) > 0)
    def _():
        for at, part in zip(starts, parts):
            out_ref[at : at + part.shape[0], :] += part


def half_terms(half, prod_at, hc_edge, hp_edge, delta, products, tile=2048):
    count, width = delta.shape
    tile = min(tile, count)
    columns = width // 2
    rows = products // 2 + 2 * columns
    edge = pl.BlockSpec((tile, columns), lambda i, h: (i, h[0]))
    return pl.pallas_call(
        terms_kernel,
        grid_spec=pltpu.PrefetchScalarGridSpec(
            num_scalar_prefetch=1,
            grid=(count // tile,),
            in_specs=[
                pl.BlockSpec((1, tile), lambda i, h: (0, i)),
                edge,
                edge,
                pl.BlockSpec((tile, width), lambda i, h: (i, 0)),
            ],
            out_specs=pl.BlockSpec((rows, width), lambda i, h: (0, 0)),
        ),
        out_shape=jax.ShapeDtypeStruct((rows, width), jnp.float32),
        compiler_params=pltpu.CompilerParams(vmem_limit_bytes=32 << 20),
        cost_estimate=pl.CostEstimate(
            flops=2 * count * rows * width, bytes_accessed=4 * count * width, transcendentals=0
        ),
        name="half_terms",
    )(half.reshape(1), prod_at.reshape(1, count), hc_edge, hp_edge, delta)


def owner_sum_kernel(key_ref, rows_ref, *refs):
    out_ref = refs[-1]
    tile = out_ref.shape[0]
    wanted = pl.program_id(0) * tile + lax.broadcasted_iota(jnp.int32, (tile, 1), 0)
    hot = jnp.where(key_ref[...] == wanted, jnp.bfloat16(1), jnp.bfloat16(0))
    out_ref[...] = jnp.dot(hot, rows_ref[...], preferred_element_type=jnp.float32)


def owner_sum(keys, rows, owned, width, at, earlier=None, tile=512):
    count, columns = rows.shape
    tile = min(tile, owned)
    in_specs = [
        pl.BlockSpec((1, count), lambda i: (0, 0)),
        pl.BlockSpec((count, columns), lambda i: (0, 0)),
    ]
    operands = [keys.reshape(1, count), rows]
    aliases = {}
    if earlier is not None:
        in_specs.append(pl.BlockSpec(memory_space=pl.ANY))
        operands.append(earlier)
        aliases = {2: 0}
    return pl.pallas_call(
        owner_sum_kernel,
        grid=(owned // tile,),
        out_shape=jax.ShapeDtypeStruct((owned, width), jnp.float32),
        in_specs=in_specs,
        out_specs=pl.BlockSpec((tile, columns), lambda i: (i, at // columns)),
        input_output_aliases=aliases,
        compiler_params=pltpu.CompilerParams(vmem_limit_bytes=32 << 20),
        cost_estimate=pl.CostEstimate(
            flops=0 if earlier is None else 2 * owned * columns * count,
            bytes_accessed=0 if earlier is None else 2 * count * columns + 4 * owned * columns,
            transcendentals=0,
        ),
        name="owner_sum",
    )(*operands)


def delta_kernel(got_ref, product_ref, gate_ref, weight_ref, delta_ref, *out_refs):
    upstream = got_ref[...].astype(jnp.float32) + product_ref[...].astype(jnp.float32)
    delta = (upstream * gate_ref[...]).astype(jnp.bfloat16)
    delta_ref[...] = delta
    at = 0
    for out_ref in out_refs:
        part = weight_ref[at : at + out_ref.shape[1], :]
        at += out_ref.shape[1]
        out_ref[...] = lax.dot_general(
            delta, part, (((1,), (1,)), ((), ())), preferred_element_type=jnp.float32
        ).astype(jnp.bfloat16)


def delta_and_rows(got, product_rows, gate, weight, cuts, tile=1024):
    count, width = got.shape
    tile = min(tile, count)
    slots = lambda columns: pl.BlockSpec((tile, columns), lambda i: (i, 0))
    return pl.pallas_call(
        delta_kernel,
        grid=(count // tile,),
        in_specs=[
            slots(width),
            slots(width),
            slots(width),
            pl.BlockSpec((width, width), lambda i: (0, 0)),
        ],
        out_specs=[slots(width)] + [slots(columns) for columns in cuts],
        out_shape=[jax.ShapeDtypeStruct((count, width), jnp.bfloat16)]
        + [pltpu.HBM((count, columns), jnp.bfloat16) for columns in cuts],
        compiler_params=pltpu.CompilerParams(vmem_limit_bytes=56 << 20),
        cost_estimate=pl.CostEstimate(
            flops=2 * count * width * width, bytes_accessed=12 * count * width, transcendentals=0
        ),
        name="delta_and_rows",
    )(got, product_rows, gate, weight)


def place():
    row = lax.axis_index("rows")
    return row % 2, row // 2, lax.axis_index("grp")


def spread(mine, shift, size, step, here):
    blocks = [mine] + [shift(mine, step * k) for k in range(1, size)]
    stacked = jnp.zeros((size,) + mine.shape, mine.dtype)
    for k, block in enumerate(blocks):
        stacked = lax.dynamic_update_index_in_dim(stacked, block, here ^ k, 0)
    return stacked


def gather_grp(mine):
    return spread(mine, shift_grp, lax.axis_size("grp"), 1, lax.axis_index("grp"))


def gather_rows(own):
    core, plane, grp = place()
    own = spread(own, shift_rows, lax.axis_size("rows") // 2, 2, plane)
    other = shift_rows(own, 1)
    first = core == 0
    return jnp.stack([jnp.where(first, own, other), jnp.where(first, other, own)])


def fold(terms, shift, size, step, here):
    total = lax.dynamic_index_in_dim(terms, here, 0, False)
    leaving = terms.astype(jnp.bfloat16)
    for k in range(1, size):
        sent = lax.dynamic_index_in_dim(leaving, here ^ k, 0, False)
        total = total + shift(sent, step * k).astype(jnp.float32)
    return total


def body(hc_edge, hp_edge, cust_count, recv_key, prod_key, cust_grad, prod_grad, w_cust, w_prod):
    devices = lax.axis_size(AXES)
    grps = lax.axis_size("grp")
    planes = lax.axis_size("rows") // 2
    slot_count, width = hc_edge.shape
    capacity = slot_count // devices
    product_count = prod_grad.shape[0]
    grid = (2, planes, grps)

    products = gather_grp(prod_grad)
    owned_rows = pick(cust_grad, recv_key, pltpu.HBM, 60)
    owned_rows, products = lax.optimization_barrier((owned_rows, products))
    fetched = lax.all_to_all(
        owned_rows.reshape(devices, capacity, width), AXES, split_axis=0, concat_axis=0, tiled=True
    ).reshape(slot_count, width)

    owner, low = prod_key // product_count, prod_key % product_count
    row, grp = owner // grps, owner % grps
    prod_at = (((row % 2) * planes + row // 2) * grps + grp) * product_count + low
    product_table = gather_rows(products).reshape(devices * product_count, width)
    product_rows = pick(product_table, prod_at, jax.ShapeDtypeStruct, 16)

    gate = slot_gate(cust_count, hc_edge, hp_edge, w_cust, w_prod)
    cut = width // 2
    delta, first, second = delta_and_rows(
        fetched, product_rows, gate, w_cust, (cut, width - cut)
    )

    def give_back(rows):
        return lax.all_to_all(
            rows.reshape(devices, capacity, -1), AXES, split_axis=0, concat_axis=0, tiled=True
        ).reshape(slot_count, -1)

    returned = give_back(first)

    core, plane, _ = place()
    products = devices * product_count
    sent = half_terms(1 - core, prod_at, hc_edge, hp_edge, delta, products)
    kept = half_terms(core, prod_at, hc_edge, hp_edge, delta, products)
    kept = kept + shift_rows(sent, 1)
    cuts = (0, products // 2, products // 2 + width // 2, products // 2 + width)
    terms = jnp.concatenate(
        [kept[a:b].reshape(planes, grps, -1, width) for a, b in zip(cuts, cuts[1:])], axis=2
    )
    leaving = terms.astype(jnp.bfloat16)
    got = [
        shift_rows(lax.dynamic_index_in_dim(leaving, plane ^ k, 0, False), 2 * k)
        for k in range(1, planes)
    ]
    got, returned = lax.optimization_barrier((got, returned))
    mine = lax.dynamic_index_in_dim(terms, plane, 0, False)
    for block in got:
        mine = mine + block.astype(jnp.float32)
    mine = fold(mine, shift_grp, grps, 1, lax.axis_index("grp"))
    mine, second = lax.optimization_barrier((mine, second))
    returned_second = give_back(second)
    grad_scale = 1.0 / math.sqrt(slot_count * devices)
    share = width // devices
    owned = cust_grad.shape[0]
    own = gather_grp(mine[product_count:].astype(jnp.bfloat16))
    own, mine, returned = lax.optimization_barrier((own, mine, returned))
    prod_table_grad = lax.dot_general(
        mine[:product_count],
        w_prod.astype(jnp.float32),
        (((1,), (1,)), ((), ())),
        precision=lax.Precision.HIGHEST,
        preferred_element_type=jnp.float32,
    ) * math.sqrt(product_count / slot_count)
    table = owner_sum(recv_key, returned, owned, width, 0)
    own = spread(own, shift_rows, planes, 2, plane)
    own, table, prod_table_grad = lax.optimization_barrier((own, table, prod_table_grad))
    other = shift_rows(own, 1)
    cust_table_grad = owner_sum(recv_key, returned_second, owned, width, cut, table)

    def whole(share_at):
        pick_share = slice(share_at, share_at + share)
        mine_part, other_part = own[:, :, pick_share], other[:, :, pick_share]
        first = lax.axis_index("rows") % 2 == 0
        both = [jnp.where(first, mine_part, other_part), jnp.where(first, other_part, mine_part)]
        return jnp.stack(both).astype(jnp.float32).reshape(width, width) * grad_scale

    return cust_table_grad, prod_table_grad, whole(0), whole(share)


def solution(mesh):
    rows = P(AXES, None)
    placed = (rows, rows, rows, P(AXES), P(AXES), rows, rows, P(), P())
    return jax.shard_map(
        body,
        mesh=mesh,
        in_specs=placed,
        out_specs=(rows, rows, P(), P()),
        check_vma=False,
    )
```

```python
import functools
import math

import jax
import jax.numpy as jnp
from jax import lax
from jax.experimental import pallas as pl
from jax.experimental.pallas import tpu as pltpu
from jax.sharding import PartitionSpec as P

AXES = ("rows", "grp")


def shift_rows(value, mask):
    size = lax.axis_size("rows")
    return lax.ppermute(value, "rows", [(i, i ^ mask) for i in range(size)])


def shift_grp(value, mask):
    size = lax.axis_size("grp")
    return lax.ppermute(value, "grp", [(i, i ^ mask) for i in range(size)])


def pick_kernel(key_ref, table_ref, out_ref):
    tile, length = key_ref.shape[1], table_ref.shape[0]
    keys = jnp.transpose(jnp.broadcast_to(key_ref[...], (128, tile)))
    lane = lax.broadcasted_iota(jnp.int32, (tile, 128), 1)
    one, zero = jnp.bfloat16(1), jnp.bfloat16(0)
    hot = jnp.concatenate(
        [jnp.where(keys == lane + at, one, zero) for at in range(0, length, 128)], axis=1
    )
    out_ref[...] = jnp.dot(hot, table_ref[...], preferred_element_type=jnp.float32).astype(
        jnp.bfloat16
    )


def pick(table, keys, space, limit, tile=1024):
    length, width = table.shape
    count = keys.shape[0]
    tile = min(tile, count)
    return pl.pallas_call(
        pick_kernel,
        grid=(count // tile,),
        out_shape=space((count, width), jnp.bfloat16),
        in_specs=[
            pl.BlockSpec((1, tile), lambda i: (0, i)),
            pl.BlockSpec((length, width), lambda i: (0, 0)),
        ],
        out_specs=pl.BlockSpec((tile, width), lambda i: (i, 0)),
        compiler_params=pltpu.CompilerParams(vmem_limit_bytes=limit << 20),
        cost_estimate=pl.CostEstimate(
            flops=2 * count * length * width,
            bytes_accessed=2 * (length + count) * width,
            transcendentals=0,
        ),
        name="pick_rows",
    )(keys.reshape(1, count), table)


def gate_kernel(count_ref, hc_ref, hp_ref, wc_ref, wp_ref, out_ref, *, capacity):
    blocks = out_ref.shape[0] // capacity
    preact = jnp.dot(hc_ref[...], wc_ref[...], preferred_element_type=jnp.float32) + jnp.dot(
        hp_ref[...], wp_ref[...], preferred_element_type=jnp.float32
    )
    squashed = jax.nn.sigmoid(preact)
    slot = lax.broadcasted_iota(jnp.int32, (capacity, 1), 0)
    first = pl.program_id(0) * blocks
    live = jnp.concatenate([slot < count_ref[0, first + k] for k in range(blocks)])
    out_ref[...] = jnp.where(live, squashed * (1.0 + preact * (1.0 - squashed)), 0.0)


def slot_gate(cust_count, hc_edge, hp_edge, w_cust, w_prod, tile=512):
    count, width = hc_edge.shape
    tile = min(tile, count)
    slots = pl.BlockSpec((tile, width), lambda i, c: (i, 0))
    whole = pl.BlockSpec((width, width), lambda i, c: (0, 0))
    return pl.pallas_call(
        functools.partial(gate_kernel, capacity=count // cust_count.shape[1]),
        grid_spec=pltpu.PrefetchScalarGridSpec(
            num_scalar_prefetch=1,
            grid=(count // tile,),
            in_specs=[slots, slots, whole, whole],
            out_specs=slots,
        ),
        out_shape=pltpu.VMEM((count, width), jnp.float32),
        compiler_params=pltpu.CompilerParams(vmem_limit_bytes=32 << 20),
        cost_estimate=pl.CostEstimate(
            flops=4 * count * width * width,
            bytes_accessed=8 * count * width,
            transcendentals=count * width,
        ),
        name="slot_gate",
    )(cust_count, hc_edge, hp_edge, w_cust, w_prod)


def terms_kernel(half_ref, at_ref, hc_ref, hp_ref, delta_ref, out_ref):
    delta = delta_ref[...]
    columns = hc_ref.shape[1]
    products = out_ref.shape[0] - 2 * columns
    wanted = half_ref[0] * products + lax.broadcasted_iota(jnp.int32, (products, 1), 0)
    hot = jnp.where(at_ref[...] == wanted, jnp.bfloat16(1), jnp.bfloat16(0))
    contract = (((0,), (0,)), ((), ()))
    parts = (
        jnp.dot(hot, delta, preferred_element_type=jnp.float32),
        lax.dot_general(hc_ref[...], delta, contract, preferred_element_type=jnp.float32),
        lax.dot_general(hp_ref[...], delta, contract, preferred_element_type=jnp.float32),
    )
    starts = (0, products, products + columns)

    @pl.when(pl.program_id(0) == 0)
    def _():
        for at, part in zip(starts, parts):
            out_ref[at : at + part.shape[0], :] = part

    @pl.when(pl.program_id(0) > 0)
    def _():
        for at, part in zip(starts, parts):
            out_ref[at : at + part.shape[0], :] += part


def half_terms(half, prod_at, hc_edge, hp_edge, delta, products, tile=2048):
    count, width = delta.shape
    tile = min(tile, count)
    columns = width // 2
    rows = products // 2 + 2 * columns
    edge = pl.BlockSpec((tile, columns), lambda i, h: (i, h[0]))
    return pl.pallas_call(
        terms_kernel,
        grid_spec=pltpu.PrefetchScalarGridSpec(
            num_scalar_prefetch=1,
            grid=(count // tile,),
            in_specs=[
                pl.BlockSpec((1, tile), lambda i, h: (0, i)),
                edge,
                edge,
                pl.BlockSpec((tile, width), lambda i, h: (i, 0)),
            ],
            out_specs=pl.BlockSpec((rows, width), lambda i, h: (0, 0)),
        ),
        out_shape=jax.ShapeDtypeStruct((rows, width), jnp.float32),
        compiler_params=pltpu.CompilerParams(vmem_limit_bytes=32 << 20),
        cost_estimate=pl.CostEstimate(
            flops=2 * count * rows * width, bytes_accessed=4 * count * width, transcendentals=0
        ),
        name="half_terms",
    )(half.reshape(1), prod_at.reshape(1, count), hc_edge, hp_edge, delta)


def owner_sum_kernel(key_ref, rows_ref, *refs):
    out_ref = refs[-1]
    tile = out_ref.shape[0]
    wanted = pl.program_id(0) * tile + lax.broadcasted_iota(jnp.int32, (tile, 1), 0)
    hot = jnp.where(key_ref[...] == wanted, jnp.bfloat16(1), jnp.bfloat16(0))
    out_ref[...] = jnp.dot(hot, rows_ref[...], preferred_element_type=jnp.float32)


def owner_sum(keys, rows, owned, width, at, earlier=None, tile=1024):
    count, columns = rows.shape
    tile = min(tile, owned)
    in_specs = [
        pl.BlockSpec((1, count), lambda i: (0, 0)),
        pl.BlockSpec((count, columns), lambda i: (0, 0)),
    ]
    operands = [keys.reshape(1, count), rows]
    aliases = {}
    if earlier is not None:
        in_specs.append(pl.BlockSpec(memory_space=pl.ANY))
        operands.append(earlier)
        aliases = {2: 0}
    return pl.pallas_call(
        owner_sum_kernel,
        grid=(owned // tile,),
        out_shape=jax.ShapeDtypeStruct((owned, width), jnp.float32),
        in_specs=in_specs,
        out_specs=pl.BlockSpec((tile, columns), lambda i: (i, at // columns)),
        input_output_aliases=aliases,
        compiler_params=pltpu.CompilerParams(vmem_limit_bytes=32 << 20),
        cost_estimate=pl.CostEstimate(
            flops=0 if earlier is None else 2 * owned * columns * count,
            bytes_accessed=0 if earlier is None else 2 * count * columns + 4 * owned * columns,
            transcendentals=0,
        ),
        name="owner_sum",
    )(*operands)


def delta_kernel(got_ref, product_ref, gate_ref, weight_ref, delta_ref, *out_refs):
    upstream = got_ref[...].astype(jnp.float32) + product_ref[...].astype(jnp.float32)
    delta = (upstream * gate_ref[...]).astype(jnp.bfloat16)
    delta_ref[...] = delta
    at = 0
    for out_ref in out_refs:
        part = weight_ref[at : at + out_ref.shape[1], :]
        at += out_ref.shape[1]
        out_ref[...] = lax.dot_general(
            delta, part, (((1,), (1,)), ((), ())), preferred_element_type=jnp.float32
        ).astype(jnp.bfloat16)


def delta_and_rows(got, product_rows, gate, weight, cuts, tile=1024):
    count, width = got.shape
    tile = min(tile, count)
    slots = lambda columns: pl.BlockSpec((tile, columns), lambda i: (i, 0))
    return pl.pallas_call(
        delta_kernel,
        grid=(count // tile,),
        in_specs=[
            slots(width),
            slots(width),
            slots(width),
            pl.BlockSpec((width, width), lambda i: (0, 0)),
        ],
        out_specs=[slots(width)] + [slots(columns) for columns in cuts],
        out_shape=[jax.ShapeDtypeStruct((count, width), jnp.bfloat16)]
        + [pltpu.HBM((count, columns), jnp.bfloat16) for columns in cuts],
        compiler_params=pltpu.CompilerParams(vmem_limit_bytes=56 << 20),
        cost_estimate=pl.CostEstimate(
            flops=2 * count * width * width, bytes_accessed=12 * count * width, transcendentals=0
        ),
        name="delta_and_rows",
    )(got, product_rows, gate, weight)


def place():
    row = lax.axis_index("rows")
    return row % 2, row // 2, lax.axis_index("grp")


def spread(mine, shift, size, step, here):
    blocks = [mine] + [shift(mine, step * k) for k in range(1, size)]
    stacked = jnp.zeros((size,) + mine.shape, mine.dtype)
    for k, block in enumerate(blocks):
        stacked = lax.dynamic_update_index_in_dim(stacked, block, here ^ k, 0)
    return stacked


def gather_grp(mine):
    return spread(mine, shift_grp, lax.axis_size("grp"), 1, lax.axis_index("grp"))


def gather_rows(own):
    core, plane, grp = place()
    own = spread(own, shift_rows, lax.axis_size("rows") // 2, 2, plane)
    other = shift_rows(own, 1)
    first = core == 0
    return jnp.stack([jnp.where(first, own, other), jnp.where(first, other, own)])


def fold(terms, shift, size, step, here):
    total = lax.dynamic_index_in_dim(terms, here, 0, False)
    leaving = terms.astype(jnp.bfloat16)
    for k in range(1, size):
        sent = lax.dynamic_index_in_dim(leaving, here ^ k, 0, False)
        total = total + shift(sent, step * k).astype(jnp.float32)
    return total


def body(hc_edge, hp_edge, cust_count, recv_key, prod_key, cust_grad, prod_grad, w_cust, w_prod):
    devices = lax.axis_size(AXES)
    grps = lax.axis_size("grp")
    planes = lax.axis_size("rows") // 2
    slot_count, width = hc_edge.shape
    capacity = slot_count // devices
    product_count = prod_grad.shape[0]
    grid = (2, planes, grps)

    products = gather_grp(prod_grad)
    owned_rows = pick(cust_grad, recv_key, pltpu.HBM, 60)
    owned_rows, products = lax.optimization_barrier((owned_rows, products))
    fetched = lax.all_to_all(
        owned_rows.reshape(devices, capacity, width), AXES, split_axis=0, concat_axis=0, tiled=True
    ).reshape(slot_count, width)

    owner, low = prod_key // product_count, prod_key % product_count
    row, grp = owner // grps, owner % grps
    prod_at = (((row % 2) * planes + row // 2) * grps + grp) * product_count + low
    product_table = gather_rows(products).reshape(devices * product_count, width)
    product_rows = pick(product_table, prod_at, jax.ShapeDtypeStruct, 16)

    gate = slot_gate(cust_count, hc_edge, hp_edge, w_cust, w_prod)
    cut = width * 3 // 4
    delta, first, second = delta_and_rows(
        fetched, product_rows, gate, w_cust, (cut, width - cut)
    )

    def give_back(rows):
        return lax.all_to_all(
            rows.reshape(devices, capacity, -1), AXES, split_axis=0, concat_axis=0, tiled=True
        ).reshape(slot_count, -1)

    returned = give_back(first)

    core, plane, _ = place()
    products = devices * product_count
    sent = half_terms(1 - core, prod_at, hc_edge, hp_edge, delta, products)
    kept = half_terms(core, prod_at, hc_edge, hp_edge, delta, products)
    kept = kept + shift_rows(sent, 1)
    cuts = (0, products // 2, products // 2 + width // 2, products // 2 + width)
    terms = jnp.concatenate(
        [kept[a:b].reshape(planes, grps, -1, width) for a, b in zip(cuts, cuts[1:])], axis=2
    )
    leaving = terms.astype(jnp.bfloat16)
    got = [
        shift_rows(lax.dynamic_index_in_dim(leaving, plane ^ k, 0, False), 2 * k)
        for k in range(1, planes)
    ]
    mine = lax.dynamic_index_in_dim(terms, plane, 0, False)
    for block in got:
        mine = mine + block.astype(jnp.float32)
    mine = fold(mine, shift_grp, grps, 1, lax.axis_index("grp"))
    mine, returned, second = lax.optimization_barrier((mine, returned, second))
    returned_second = give_back(second)
    grad_scale = 1.0 / math.sqrt(slot_count * devices)
    share = width // devices
    owned = cust_grad.shape[0]
    own = gather_grp(mine[product_count:].astype(jnp.bfloat16))
    own, mine, returned = lax.optimization_barrier((own, mine, returned))
    prod_table_grad = lax.dot_general(
        mine[:product_count],
        w_prod.astype(jnp.float32),
        (((1,), (1,)), ((), ())),
        precision=lax.Precision.HIGHEST,
        preferred_element_type=jnp.float32,
    ) * math.sqrt(product_count / slot_count)
    table = owner_sum(recv_key, returned, owned, width, 0)
    own = spread(own, shift_rows, planes, 2, plane)
    own, table, prod_table_grad = lax.optimization_barrier((own, table, prod_table_grad))
    other = shift_rows(own, 1)
    cust_table_grad = owner_sum(recv_key, returned_second, owned, width, cut, table)
    other, cust_table_grad = lax.optimization_barrier((other, cust_table_grad))

    def whole(share_at):
        pick_share = slice(share_at, share_at + share)
        mine_part, other_part = own[:, :, pick_share], other[:, :, pick_share]
        first = lax.axis_index("rows") % 2 == 0
        both = [jnp.where(first, mine_part, other_part), jnp.where(first, other_part, mine_part)]
        return jnp.stack(both).astype(jnp.float32).reshape(width, width) * grad_scale

    return cust_table_grad, prod_table_grad, whole(0), whole(share)


def solution(mesh):
    rows = P(AXES, None)
    placed = (rows, rows, rows, P(AXES), P(AXES), rows, rows, P(), P())
    return jax.shard_map(
        body,
        mesh=mesh,
        in_specs=placed,
        out_specs=(rows, rows, P(), P()),
        check_vma=False,
    )
```

```python
import functools
import math

import jax
import jax.numpy as jnp
from jax import lax
from jax.experimental import pallas as pl
from jax.experimental.pallas import tpu as pltpu
from jax.sharding import PartitionSpec as P

AXES = ("rows", "grp")


def shift_rows(value, mask):
    size = lax.axis_size("rows")
    return lax.ppermute(value, "rows", [(i, i ^ mask) for i in range(size)])


def shift_grp(value, mask):
    size = lax.axis_size("grp")
    return lax.ppermute(value, "grp", [(i, i ^ mask) for i in range(size)])


def pick_kernel(key_ref, table_ref, out_ref):
    tile, length = key_ref.shape[1], table_ref.shape[0]
    keys = jnp.transpose(jnp.broadcast_to(key_ref[...], (128, tile)))
    lane = lax.broadcasted_iota(jnp.int32, (tile, 128), 1)
    one, zero = jnp.bfloat16(1), jnp.bfloat16(0)
    hot = jnp.concatenate(
        [jnp.where(keys == lane + at, one, zero) for at in range(0, length, 128)], axis=1
    )
    out_ref[...] = jnp.dot(hot, table_ref[...], preferred_element_type=jnp.float32).astype(
        jnp.bfloat16
    )


def pick(table, keys, space, limit, tile=1024):
    length, width = table.shape
    count = keys.shape[0]
    tile = min(tile, count)
    return pl.pallas_call(
        pick_kernel,
        grid=(count // tile,),
        out_shape=space((count, width), jnp.bfloat16),
        in_specs=[
            pl.BlockSpec((1, tile), lambda i: (0, i)),
            pl.BlockSpec((length, width), lambda i: (0, 0)),
        ],
        out_specs=pl.BlockSpec((tile, width), lambda i: (i, 0)),
        compiler_params=pltpu.CompilerParams(vmem_limit_bytes=limit << 20),
        cost_estimate=pl.CostEstimate(
            flops=2 * count * length * width,
            bytes_accessed=2 * (length + count) * width,
            transcendentals=0,
        ),
        name="pick_rows",
    )(keys.reshape(1, count), table)


def gate_kernel(count_ref, hc_ref, hp_ref, wc_ref, wp_ref, out_ref, *, capacity):
    blocks = out_ref.shape[0] // capacity
    preact = jnp.dot(hc_ref[...], wc_ref[...], preferred_element_type=jnp.float32) + jnp.dot(
        hp_ref[...], wp_ref[...], preferred_element_type=jnp.float32
    )
    squashed = jax.nn.sigmoid(preact)
    slot = lax.broadcasted_iota(jnp.int32, (capacity, 1), 0)
    first = pl.program_id(0) * blocks
    live = jnp.concatenate([slot < count_ref[0, first + k] for k in range(blocks)])
    out_ref[...] = jnp.where(live, squashed * (1.0 + preact * (1.0 - squashed)), 0.0)


def slot_gate(cust_count, hc_edge, hp_edge, w_cust, w_prod, tile=512):
    count, width = hc_edge.shape
    tile = min(tile, count)
    slots = pl.BlockSpec((tile, width), lambda i, c: (i, 0))
    whole = pl.BlockSpec((width, width), lambda i, c: (0, 0))
    return pl.pallas_call(
        functools.partial(gate_kernel, capacity=count // cust_count.shape[1]),
        grid_spec=pltpu.PrefetchScalarGridSpec(
            num_scalar_prefetch=1,
            grid=(count // tile,),
            in_specs=[slots, slots, whole, whole],
            out_specs=slots,
        ),
        out_shape=pltpu.VMEM((count, width), jnp.float32),
        compiler_params=pltpu.CompilerParams(vmem_limit_bytes=32 << 20),
        cost_estimate=pl.CostEstimate(
            flops=4 * count * width * width,
            bytes_accessed=8 * count * width,
            transcendentals=count * width,
        ),
        name="slot_gate",
    )(cust_count, hc_edge, hp_edge, w_cust, w_prod)


def terms_kernel(half_ref, at_ref, hc_ref, hp_ref, delta_ref, out_ref):
    delta = delta_ref[...]
    columns = hc_ref.shape[1]
    products = out_ref.shape[0] - 2 * columns
    wanted = half_ref[0] * products + lax.broadcasted_iota(jnp.int32, (products, 1), 0)
    hot = jnp.where(at_ref[...] == wanted, jnp.bfloat16(1), jnp.bfloat16(0))
    contract = (((0,), (0,)), ((), ()))
    parts = (
        jnp.dot(hot, delta, preferred_element_type=jnp.float32),
        lax.dot_general(hc_ref[...], delta, contract, preferred_element_type=jnp.float32),
        lax.dot_general(hp_ref[...], delta, contract, preferred_element_type=jnp.float32),
    )
    starts = (0, products, products + columns)

    @pl.when(pl.program_id(0) == 0)
    def _():
        for at, part in zip(starts, parts):
            out_ref[at : at + part.shape[0], :] = part

    @pl.when(pl.program_id(0) > 0)
    def _():
        for at, part in zip(starts, parts):
            out_ref[at : at + part.shape[0], :] += part


def half_terms(half, prod_at, hc_edge, hp_edge, delta, products, tile=2048):
    count, width = delta.shape
    tile = min(tile, count)
    columns = width // 2
    rows = products // 2 + 2 * columns
    edge = pl.BlockSpec((tile, columns), lambda i, h: (i, h[0]))
    return pl.pallas_call(
        terms_kernel,
        grid_spec=pltpu.PrefetchScalarGridSpec(
            num_scalar_prefetch=1,
            grid=(count // tile,),
            in_specs=[
                pl.BlockSpec((1, tile), lambda i, h: (0, i)),
                edge,
                edge,
                pl.BlockSpec((tile, width), lambda i, h: (i, 0)),
            ],
            out_specs=pl.BlockSpec((rows, width), lambda i, h: (0, 0)),
        ),
        out_shape=jax.ShapeDtypeStruct((rows, width), jnp.float32),
        compiler_params=pltpu.CompilerParams(vmem_limit_bytes=32 << 20),
        cost_estimate=pl.CostEstimate(
            flops=2 * count * rows * width, bytes_accessed=4 * count * width, transcendentals=0
        ),
        name="half_terms",
    )(half.reshape(1), prod_at.reshape(1, count), hc_edge, hp_edge, delta)


def owner_sum_kernel(key_ref, rows_ref, *refs):
    out_ref = refs[-1]
    tile = out_ref.shape[0]
    wanted = pl.program_id(0) * tile + lax.broadcasted_iota(jnp.int32, (tile, 1), 0)
    hot = jnp.where(key_ref[...] == wanted, jnp.bfloat16(1), jnp.bfloat16(0))
    out_ref[...] = jnp.dot(hot, rows_ref[...], preferred_element_type=jnp.float32)


def owner_sum(keys, rows, owned, width, at, earlier=None, tile=1024):
    count, columns = rows.shape
    tile = min(tile, owned)
    in_specs = [
        pl.BlockSpec((1, count), lambda i: (0, 0)),
        pl.BlockSpec((count, columns), lambda i: (0, 0)),
    ]
    operands = [keys.reshape(1, count), rows]
    aliases = {}
    if earlier is not None:
        in_specs.append(pl.BlockSpec(memory_space=pl.ANY))
        operands.append(earlier)
        aliases = {2: 0}
    return pl.pallas_call(
        owner_sum_kernel,
        grid=(owned // tile,),
        out_shape=jax.ShapeDtypeStruct((owned, width), jnp.float32),
        in_specs=in_specs,
        out_specs=pl.BlockSpec((tile, columns), lambda i: (i, at // columns)),
        input_output_aliases=aliases,
        compiler_params=pltpu.CompilerParams(vmem_limit_bytes=32 << 20),
        cost_estimate=pl.CostEstimate(
            flops=0 if earlier is None else 2 * owned * columns * count,
            bytes_accessed=0 if earlier is None else 2 * count * columns + 4 * owned * columns,
            transcendentals=0,
        ),
        name="owner_sum",
    )(*operands)


def delta_kernel(got_ref, product_ref, gate_ref, weight_ref, delta_ref, *out_refs):
    upstream = got_ref[...].astype(jnp.float32) + product_ref[...].astype(jnp.float32)
    delta = (upstream * gate_ref[...]).astype(jnp.bfloat16)
    delta_ref[...] = delta
    at = 0
    for out_ref in out_refs:
        part = weight_ref[at : at + out_ref.shape[1], :]
        at += out_ref.shape[1]
        out_ref[...] = lax.dot_general(
            delta, part, (((1,), (1,)), ((), ())), preferred_element_type=jnp.float32
        ).astype(jnp.bfloat16)


def delta_and_rows(got, product_rows, gate, weight, cuts, tile=1024):
    count, width = got.shape
    tile = min(tile, count)
    slots = lambda columns: pl.BlockSpec((tile, columns), lambda i: (i, 0))
    return pl.pallas_call(
        delta_kernel,
        grid=(count // tile,),
        in_specs=[
            slots(width),
            slots(width),
            slots(width),
            pl.BlockSpec((width, width), lambda i: (0, 0)),
        ],
        out_specs=[slots(width)] + [slots(columns) for columns in cuts],
        out_shape=[jax.ShapeDtypeStruct((count, width), jnp.bfloat16)]
        + [pltpu.HBM((count, columns), jnp.bfloat16) for columns in cuts],
        compiler_params=pltpu.CompilerParams(vmem_limit_bytes=56 << 20),
        cost_estimate=pl.CostEstimate(
            flops=2 * count * width * width, bytes_accessed=12 * count * width, transcendentals=0
        ),
        name="delta_and_rows",
    )(got, product_rows, gate, weight)


def place():
    row = lax.axis_index("rows")
    return row % 2, row // 2, lax.axis_index("grp")


def spread(mine, shift, size, step, here):
    blocks = [mine] + [shift(mine, step * k) for k in range(1, size)]
    stacked = jnp.zeros((size,) + mine.shape, mine.dtype)
    for k, block in enumerate(blocks):
        stacked = lax.dynamic_update_index_in_dim(stacked, block, here ^ k, 0)
    return stacked


def gather_grp(mine):
    return spread(mine, shift_grp, lax.axis_size("grp"), 1, lax.axis_index("grp"))


def gather_rows(own):
    core, plane, grp = place()
    own = spread(own, shift_rows, lax.axis_size("rows") // 2, 2, plane)
    other = shift_rows(own, 1)
    first = core == 0
    return jnp.stack([jnp.where(first, own, other), jnp.where(first, other, own)])


def fold(terms, shift, size, step, here):
    total = lax.dynamic_index_in_dim(terms, here, 0, False)
    leaving = terms.astype(jnp.bfloat16)
    for k in range(1, size):
        sent = lax.dynamic_index_in_dim(leaving, here ^ k, 0, False)
        total = total + shift(sent, step * k).astype(jnp.float32)
    return total


def body(hc_edge, hp_edge, cust_count, recv_key, prod_key, cust_grad, prod_grad, w_cust, w_prod):
    devices = lax.axis_size(AXES)
    grps = lax.axis_size("grp")
    planes = lax.axis_size("rows") // 2
    slot_count, width = hc_edge.shape
    capacity = slot_count // devices
    product_count = prod_grad.shape[0]
    grid = (2, planes, grps)

    products = gather_grp(prod_grad)
    owned_rows = pick(cust_grad, recv_key, pltpu.HBM, 60)
    owned_rows, products = lax.optimization_barrier((owned_rows, products))
    fetched = lax.all_to_all(
        owned_rows.reshape(devices, capacity, width), AXES, split_axis=0, concat_axis=0, tiled=True
    ).reshape(slot_count, width)

    owner, low = prod_key // product_count, prod_key % product_count
    row, grp = owner // grps, owner % grps
    prod_at = (((row % 2) * planes + row // 2) * grps + grp) * product_count + low
    product_table = gather_rows(products).reshape(devices * product_count, width)
    product_rows = pick(product_table, prod_at, jax.ShapeDtypeStruct, 16)

    gate = slot_gate(cust_count, hc_edge, hp_edge, w_cust, w_prod)
    cut = width * 3 // 4
    delta, first, second = delta_and_rows(
        fetched, product_rows, gate, w_cust, (cut, width - cut)
    )

    def give_back(rows):
        return lax.all_to_all(
            rows.reshape(devices, capacity, -1), AXES, split_axis=0, concat_axis=0, tiled=True
        ).reshape(slot_count, -1)

    returned = give_back(first)

    core, plane, _ = place()
    products = devices * product_count
    sent = half_terms(1 - core, prod_at, hc_edge, hp_edge, delta, products)
    kept = half_terms(core, prod_at, hc_edge, hp_edge, delta, products)
    kept = kept + shift_rows(sent, 1)
    cuts = (0, products // 2, products // 2 + width // 2, products // 2 + width)
    terms = jnp.concatenate(
        [kept[a:b].reshape(planes, grps, -1, width) for a, b in zip(cuts, cuts[1:])], axis=2
    )
    leaving = terms.astype(jnp.bfloat16)
    got = [
        shift_rows(lax.dynamic_index_in_dim(leaving, plane ^ k, 0, False), 2 * k)
        for k in range(1, planes)
    ]
    mine = lax.dynamic_index_in_dim(terms, plane, 0, False)
    for block in got:
        mine = mine + block.astype(jnp.float32)
    here = lax.axis_index("grp")
    sums, weights = mine[:, :product_count], mine[:, product_count:].astype(jnp.bfloat16)
    every = weights.reshape(-1, width)
    own_sum = lax.dynamic_index_in_dim(sums, here, 0, False)
    blocks = [
        shift_grp(
            jnp.concatenate(
                [lax.dynamic_index_in_dim(sums, here ^ k, 0, False).astype(jnp.bfloat16), every]
            ),
            k,
        )
        for k in range(1, grps)
    ]
    blocks, returned = lax.optimization_barrier((blocks, returned))
    terms = [weights.astype(jnp.float32)]
    for block in blocks:
        own_sum = own_sum + block[:product_count].astype(jnp.float32)
        terms.append(block[product_count:].astype(jnp.float32).reshape(weights.shape))
    while len(terms) > 1:
        terms = [a + b for a, b in zip(terms[::2], terms[1::2])]
    own = terms[0].astype(jnp.bfloat16)
    returned_second = give_back(second)
    grad_scale = 1.0 / math.sqrt(slot_count * devices)
    share = width // devices
    owned = cust_grad.shape[0]
    prod_table_grad = lax.dot_general(
        own_sum,
        w_prod.astype(jnp.float32),
        (((1,), (1,)), ((), ())),
        precision=lax.Precision.HIGHEST,
        preferred_element_type=jnp.float32,
    ) * math.sqrt(product_count / slot_count)
    table = owner_sum(recv_key, returned, owned, width, 0)
    own = spread(own, shift_rows, planes, 2, plane)
    own, table, prod_table_grad = lax.optimization_barrier((own, table, prod_table_grad))
    other = shift_rows(own, 1)
    cust_table_grad = owner_sum(recv_key, returned_second, owned, width, cut, table)
    other, cust_table_grad = lax.optimization_barrier((other, cust_table_grad))

    def whole(share_at):
        pick_share = slice(share_at, share_at + share)
        mine_part, other_part = own[:, :, pick_share], other[:, :, pick_share]
        first = lax.axis_index("rows") % 2 == 0
        both = [jnp.where(first, mine_part, other_part), jnp.where(first, other_part, mine_part)]
        return jnp.stack(both).astype(jnp.float32).reshape(width, width) * grad_scale

    return cust_table_grad, prod_table_grad, whole(0), whole(share)


def solution(mesh):
    rows = P(AXES, None)
    placed = (rows, rows, rows, P(AXES), P(AXES), rows, rows, P(), P())
    return jax.shard_map(
        body,
        mesh=mesh,
        in_specs=placed,
        out_specs=(rows, rows, P(), P()),
        check_vma=False,
    )
```

```python
import functools
import math

import jax
import jax.numpy as jnp
from jax import lax
from jax.experimental import pallas as pl
from jax.experimental.pallas import tpu as pltpu
from jax.sharding import PartitionSpec as P

AXES = ("rows", "grp")


def shift_rows(value, mask):
    size = lax.axis_size("rows")
    return lax.ppermute(value, "rows", [(i, i ^ mask) for i in range(size)])


def shift_grp(value, mask):
    size = lax.axis_size("grp")
    return lax.ppermute(value, "grp", [(i, i ^ mask) for i in range(size)])


def pick_kernel(key_ref, table_ref, out_ref):
    tile, length = key_ref.shape[1], table_ref.shape[0]
    keys = jnp.transpose(jnp.broadcast_to(key_ref[...], (128, tile)))
    lane = lax.broadcasted_iota(jnp.int32, (tile, 128), 1)
    one, zero = jnp.bfloat16(1), jnp.bfloat16(0)
    hot = jnp.concatenate(
        [jnp.where(keys == lane + at, one, zero) for at in range(0, length, 128)], axis=1
    )
    out_ref[...] = jnp.dot(hot, table_ref[...], preferred_element_type=jnp.float32).astype(
        jnp.bfloat16
    )


def pick(table, keys, space, limit, tile=1024):
    length, width = table.shape
    count = keys.shape[0]
    tile = min(tile, count)
    return pl.pallas_call(
        pick_kernel,
        grid=(count // tile,),
        out_shape=space((count, width), jnp.bfloat16),
        in_specs=[
            pl.BlockSpec((1, tile), lambda i: (0, i)),
            pl.BlockSpec((length, width), lambda i: (0, 0)),
        ],
        out_specs=pl.BlockSpec((tile, width), lambda i: (i, 0)),
        compiler_params=pltpu.CompilerParams(vmem_limit_bytes=limit << 20),
        cost_estimate=pl.CostEstimate(
            flops=2 * count * length * width,
            bytes_accessed=2 * (length + count) * width,
            transcendentals=0,
        ),
        name="pick_rows",
    )(keys.reshape(1, count), table)


def gate_kernel(count_ref, hc_ref, hp_ref, wc_ref, wp_ref, out_ref, *, capacity):
    blocks = out_ref.shape[0] // capacity
    preact = jnp.dot(hc_ref[...], wc_ref[...], preferred_element_type=jnp.float32) + jnp.dot(
        hp_ref[...], wp_ref[...], preferred_element_type=jnp.float32
    )
    squashed = jax.nn.sigmoid(preact)
    slot = lax.broadcasted_iota(jnp.int32, (capacity, 1), 0)
    first = pl.program_id(0) * blocks
    live = jnp.concatenate([slot < count_ref[0, first + k] for k in range(blocks)])
    out_ref[...] = jnp.where(live, squashed * (1.0 + preact * (1.0 - squashed)), 0.0)


def slot_gate(cust_count, hc_edge, hp_edge, w_cust, w_prod, tile=512):
    count, width = hc_edge.shape
    tile = min(tile, count)
    slots = pl.BlockSpec((tile, width), lambda i, c: (i, 0))
    whole = pl.BlockSpec((width, width), lambda i, c: (0, 0))
    return pl.pallas_call(
        functools.partial(gate_kernel, capacity=count // cust_count.shape[1]),
        grid_spec=pltpu.PrefetchScalarGridSpec(
            num_scalar_prefetch=1,
            grid=(count // tile,),
            in_specs=[slots, slots, whole, whole],
            out_specs=slots,
        ),
        out_shape=pltpu.VMEM((count, width), jnp.float32),
        compiler_params=pltpu.CompilerParams(vmem_limit_bytes=32 << 20),
        cost_estimate=pl.CostEstimate(
            flops=4 * count * width * width,
            bytes_accessed=8 * count * width,
            transcendentals=count * width,
        ),
        name="slot_gate",
    )(cust_count, hc_edge, hp_edge, w_cust, w_prod)


def terms_kernel(half_ref, at_ref, hc_ref, hp_ref, delta_ref, out_ref):
    delta = delta_ref[...]
    columns = hc_ref.shape[1]
    products = out_ref.shape[0] - 2 * columns
    wanted = half_ref[0] * products + lax.broadcasted_iota(jnp.int32, (products, 1), 0)
    hot = jnp.where(at_ref[...] == wanted, jnp.bfloat16(1), jnp.bfloat16(0))
    contract = (((0,), (0,)), ((), ()))
    parts = (
        jnp.dot(hot, delta, preferred_element_type=jnp.float32),
        lax.dot_general(hc_ref[...], delta, contract, preferred_element_type=jnp.float32),
        lax.dot_general(hp_ref[...], delta, contract, preferred_element_type=jnp.float32),
    )
    starts = (0, products, products + columns)

    @pl.when(pl.program_id(0) == 0)
    def _():
        for at, part in zip(starts, parts):
            out_ref[at : at + part.shape[0], :] = part

    @pl.when(pl.program_id(0) > 0)
    def _():
        for at, part in zip(starts, parts):
            out_ref[at : at + part.shape[0], :] += part


def half_terms(half, prod_at, hc_edge, hp_edge, delta, products, tile=2048):
    count, width = delta.shape
    tile = min(tile, count)
    columns = width // 2
    rows = products // 2 + 2 * columns
    edge = pl.BlockSpec((tile, columns), lambda i, h: (i, h[0]))
    return pl.pallas_call(
        terms_kernel,
        grid_spec=pltpu.PrefetchScalarGridSpec(
            num_scalar_prefetch=1,
            grid=(count // tile,),
            in_specs=[
                pl.BlockSpec((1, tile), lambda i, h: (0, i)),
                edge,
                edge,
                pl.BlockSpec((tile, width), lambda i, h: (i, 0)),
            ],
            out_specs=pl.BlockSpec((rows, width), lambda i, h: (0, 0)),
        ),
        out_shape=jax.ShapeDtypeStruct((rows, width), jnp.float32),
        compiler_params=pltpu.CompilerParams(vmem_limit_bytes=32 << 20),
        cost_estimate=pl.CostEstimate(
            flops=2 * count * rows * width, bytes_accessed=4 * count * width, transcendentals=0
        ),
        name="half_terms",
    )(half.reshape(1), prod_at.reshape(1, count), hc_edge, hp_edge, delta)


def owner_sum_kernel(key_ref, rows_ref, *refs):
    out_ref = refs[-1]
    tile = out_ref.shape[0]
    wanted = pl.program_id(0) * tile + lax.broadcasted_iota(jnp.int32, (tile, 1), 0)
    hot = jnp.where(key_ref[...] == wanted, jnp.bfloat16(1), jnp.bfloat16(0))
    out_ref[...] = jnp.dot(hot, rows_ref[...], preferred_element_type=jnp.float32)


def owner_sum(keys, rows, owned, width, at, earlier=None, tile=1024):
    count, columns = rows.shape
    tile = min(tile, owned)
    in_specs = [
        pl.BlockSpec((1, count), lambda i: (0, 0)),
        pl.BlockSpec((count, columns), lambda i: (0, 0)),
    ]
    operands = [keys.reshape(1, count), rows]
    aliases = {}
    if earlier is not None:
        in_specs.append(pl.BlockSpec(memory_space=pl.ANY))
        operands.append(earlier)
        aliases = {2: 0}
    return pl.pallas_call(
        owner_sum_kernel,
        grid=(owned // tile,),
        out_shape=jax.ShapeDtypeStruct((owned, width), jnp.float32),
        in_specs=in_specs,
        out_specs=pl.BlockSpec((tile, columns), lambda i: (i, at // columns)),
        input_output_aliases=aliases,
        compiler_params=pltpu.CompilerParams(vmem_limit_bytes=32 << 20),
        cost_estimate=pl.CostEstimate(
            flops=0 if earlier is None else 2 * owned * columns * count,
            bytes_accessed=0 if earlier is None else 2 * count * columns + 4 * owned * columns,
            transcendentals=0,
        ),
        name="owner_sum",
    )(*operands)


def delta_kernel(keep, at, got_ref, product_ref, gate_ref, weight_ref, *out_refs):
    upstream = got_ref[...].astype(jnp.float32) + product_ref[...].astype(jnp.float32)
    delta = (upstream * gate_ref[...]).astype(jnp.bfloat16)
    if keep:
        out_refs[1][...] = delta
    out_ref = out_refs[0]
    part = weight_ref[at : at + out_ref.shape[1], :]
    out_ref[...] = lax.dot_general(
        delta, part, (((1,), (1,)), ((), ())), preferred_element_type=jnp.float32
    ).astype(jnp.bfloat16)


def delta_and_rows(got, product_rows, gate, weight, at, columns, keep, tile=1024):
    count, width = got.shape
    tile = min(tile, count)
    slots = lambda wide: pl.BlockSpec((tile, wide), lambda i: (i, 0))
    return pl.pallas_call(
        functools.partial(delta_kernel, keep, at),
        grid=(count // tile,),
        in_specs=[
            slots(width),
            slots(width),
            slots(width),
            pl.BlockSpec((width, width), lambda i: (0, 0)),
        ],
        out_specs=[slots(columns)] + [slots(width)] * keep,
        out_shape=[pltpu.HBM((count, columns), jnp.bfloat16)]
        + [jax.ShapeDtypeStruct((count, width), jnp.bfloat16)] * keep,
        compiler_params=pltpu.CompilerParams(vmem_limit_bytes=56 << 20),
        cost_estimate=pl.CostEstimate(
            flops=2 * count * width * width, bytes_accessed=12 * count * width, transcendentals=0
        ),
        name="delta_and_rows",
    )(got, product_rows, gate, weight)


def place():
    row = lax.axis_index("rows")
    return row % 2, row // 2, lax.axis_index("grp")


def spread(mine, shift, size, step, here):
    blocks = [mine] + [shift(mine, step * k) for k in range(1, size)]
    stacked = jnp.zeros((size,) + mine.shape, mine.dtype)
    for k, block in enumerate(blocks):
        stacked = lax.dynamic_update_index_in_dim(stacked, block, here ^ k, 0)
    return stacked


def gather_grp(mine):
    return spread(mine, shift_grp, lax.axis_size("grp"), 1, lax.axis_index("grp"))


def gather_rows(own):
    core, plane, grp = place()
    own = spread(own, shift_rows, lax.axis_size("rows") // 2, 2, plane)
    other = shift_rows(own, 1)
    first = core == 0
    return jnp.stack([jnp.where(first, own, other), jnp.where(first, other, own)])


def fold(terms, shift, size, step, here):
    total = lax.dynamic_index_in_dim(terms, here, 0, False)
    leaving = terms.astype(jnp.bfloat16)
    for k in range(1, size):
        sent = lax.dynamic_index_in_dim(leaving, here ^ k, 0, False)
        total = total + shift(sent, step * k).astype(jnp.float32)
    return total


def body(hc_edge, hp_edge, cust_count, recv_key, prod_key, cust_grad, prod_grad, w_cust, w_prod):
    devices = lax.axis_size(AXES)
    grps = lax.axis_size("grp")
    planes = lax.axis_size("rows") // 2
    slot_count, width = hc_edge.shape
    capacity = slot_count // devices
    product_count = prod_grad.shape[0]
    grid = (2, planes, grps)

    products = gather_grp(prod_grad)
    owned_rows = pick(cust_grad, recv_key, pltpu.HBM, 60)
    owned_rows, products = lax.optimization_barrier((owned_rows, products))
    fetched = lax.all_to_all(
        owned_rows.reshape(devices, capacity, width), AXES, split_axis=0, concat_axis=0, tiled=True
    ).reshape(slot_count, width)

    owner, low = prod_key // product_count, prod_key % product_count
    row, grp = owner // grps, owner % grps
    prod_at = (((row % 2) * planes + row // 2) * grps + grp) * product_count + low
    product_table = gather_rows(products).reshape(devices * product_count, width)
    product_rows = pick(product_table, prod_at, jax.ShapeDtypeStruct, 16)

    gate = slot_gate(cust_count, hc_edge, hp_edge, w_cust, w_prod)
    cut = width * 3 // 4
    parts = (fetched, product_rows, gate, w_cust)
    (first,) = delta_and_rows(*parts, 0, cut, False)
    second, delta = delta_and_rows(*parts, cut, width - cut, True)

    def give_back(rows):
        return lax.all_to_all(
            rows.reshape(devices, capacity, -1), AXES, split_axis=0, concat_axis=0, tiled=True
        ).reshape(slot_count, -1)

    returned = give_back(first)

    core, plane, _ = place()
    products = devices * product_count
    sent = half_terms(1 - core, prod_at, hc_edge, hp_edge, delta, products)
    kept = half_terms(core, prod_at, hc_edge, hp_edge, delta, products)
    kept = kept + shift_rows(sent, 1)
    cuts = (0, products // 2, products // 2 + width // 2, products // 2 + width)
    terms = jnp.concatenate(
        [kept[a:b].reshape(planes, grps, -1, width) for a, b in zip(cuts, cuts[1:])], axis=2
    )
    leaving = terms.astype(jnp.bfloat16)
    got = [
        shift_rows(lax.dynamic_index_in_dim(leaving, plane ^ k, 0, False), 2 * k)
        for k in range(1, planes)
    ]
    mine = lax.dynamic_index_in_dim(terms, plane, 0, False)
    for block in got:
        mine = mine + block.astype(jnp.float32)
    here = lax.axis_index("grp")
    sums, weights = mine[:, :product_count], mine[:, product_count:].astype(jnp.bfloat16)
    every = weights.reshape(-1, width)
    own_sum = lax.dynamic_index_in_dim(sums, here, 0, False)
    blocks = [
        shift_grp(
            jnp.concatenate(
                [lax.dynamic_index_in_dim(sums, here ^ k, 0, False).astype(jnp.bfloat16), every]
            ),
            k,
        )
        for k in range(1, grps)
    ]
    blocks, returned = lax.optimization_barrier((blocks, returned))
    terms = [weights.astype(jnp.float32)]
    for block in blocks:
        own_sum = own_sum + block[:product_count].astype(jnp.float32)
        terms.append(block[product_count:].astype(jnp.float32).reshape(weights.shape))
    while len(terms) > 1:
        terms = [a + b for a, b in zip(terms[::2], terms[1::2])]
    own = terms[0].astype(jnp.bfloat16)
    returned_second = give_back(second)
    grad_scale = 1.0 / math.sqrt(slot_count * devices)
    share = width // devices
    owned = cust_grad.shape[0]
    prod_table_grad = lax.dot_general(
        own_sum,
        w_prod.astype(jnp.float32),
        (((1,), (1,)), ((), ())),
        precision=lax.Precision.HIGHEST,
        preferred_element_type=jnp.float32,
    ) * math.sqrt(product_count / slot_count)
    table = owner_sum(recv_key, returned, owned, width, 0)
    own = spread(own, shift_rows, planes, 2, plane)
    own, table, prod_table_grad = lax.optimization_barrier((own, table, prod_table_grad))
    other = shift_rows(own, 1)
    cust_table_grad = owner_sum(recv_key, returned_second, owned, width, cut, table)
    other, cust_table_grad = lax.optimization_barrier((other, cust_table_grad))

    def whole(share_at):
        pick_share = slice(share_at, share_at + share)
        mine_part, other_part = own[:, :, pick_share], other[:, :, pick_share]
        first = lax.axis_index("rows") % 2 == 0
        both = [jnp.where(first, mine_part, other_part), jnp.where(first, other_part, mine_part)]
        return jnp.stack(both).astype(jnp.float32).reshape(width, width) * grad_scale

    return cust_table_grad, prod_table_grad, whole(0), whole(share)


def solution(mesh):
    rows = P(AXES, None)
    placed = (rows, rows, rows, P(AXES), P(AXES), rows, rows, P(), P())
    return jax.shard_map(
        body,
        mesh=mesh,
        in_specs=placed,
        out_specs=(rows, rows, P(), P()),
        check_vma=False,
    )
```

```python
import functools
import math

import jax
import jax.numpy as jnp
from jax import lax
from jax.experimental import pallas as pl
from jax.experimental.pallas import tpu as pltpu
from jax.sharding import PartitionSpec as P

AXES = ("rows", "grp")


def shift_rows(value, mask):
    size = lax.axis_size("rows")
    return lax.ppermute(value, "rows", [(i, i ^ mask) for i in range(size)])


def shift_grp(value, mask):
    size = lax.axis_size("grp")
    return lax.ppermute(value, "grp", [(i, i ^ mask) for i in range(size)])


def pick_kernel(key_ref, table_ref, out_ref):
    tile, length = key_ref.shape[1], table_ref.shape[0]
    keys = jnp.transpose(jnp.broadcast_to(key_ref[...], (128, tile)))
    lane = lax.broadcasted_iota(jnp.int32, (tile, 128), 1)
    one, zero = jnp.bfloat16(1), jnp.bfloat16(0)
    hot = jnp.concatenate(
        [jnp.where(keys == lane + at, one, zero) for at in range(0, length, 128)], axis=1
    )
    out_ref[...] = jnp.dot(hot, table_ref[...], preferred_element_type=jnp.float32).astype(
        jnp.bfloat16
    )


def pick(table, keys, space, limit, tile=1024):
    length, width = table.shape
    count = keys.shape[0]
    tile = min(tile, count)
    return pl.pallas_call(
        pick_kernel,
        grid=(count // tile,),
        out_shape=space((count, width), jnp.bfloat16),
        in_specs=[
            pl.BlockSpec((1, tile), lambda i: (0, i)),
            pl.BlockSpec((length, width), lambda i: (0, 0)),
        ],
        out_specs=pl.BlockSpec((tile, width), lambda i: (i, 0)),
        compiler_params=pltpu.CompilerParams(vmem_limit_bytes=limit << 20),
        cost_estimate=pl.CostEstimate(
            flops=2 * count * length * width,
            bytes_accessed=2 * (length + count) * width,
            transcendentals=0,
        ),
        name="pick_rows",
    )(keys.reshape(1, count), table)


def gate_kernel(count_ref, hc_ref, hp_ref, wc_ref, wp_ref, out_ref, *, capacity):
    blocks = out_ref.shape[0] // capacity
    preact = jnp.dot(hc_ref[...], wc_ref[...], preferred_element_type=jnp.float32) + jnp.dot(
        hp_ref[...], wp_ref[...], preferred_element_type=jnp.float32
    )
    squashed = jax.nn.sigmoid(preact)
    slot = lax.broadcasted_iota(jnp.int32, (capacity, 1), 0)
    first = pl.program_id(0) * blocks
    live = jnp.concatenate([slot < count_ref[0, first + k] for k in range(blocks)])
    out_ref[...] = jnp.where(live, squashed * (1.0 + preact * (1.0 - squashed)), 0.0)


def slot_gate(cust_count, hc_edge, hp_edge, w_cust, w_prod, tile=512):
    count, width = hc_edge.shape
    tile = min(tile, count)
    slots = pl.BlockSpec((tile, width), lambda i, c: (i, 0))
    whole = pl.BlockSpec((width, width), lambda i, c: (0, 0))
    return pl.pallas_call(
        functools.partial(gate_kernel, capacity=count // cust_count.shape[1]),
        grid_spec=pltpu.PrefetchScalarGridSpec(
            num_scalar_prefetch=1,
            grid=(count // tile,),
            in_specs=[slots, slots, whole, whole],
            out_specs=slots,
        ),
        out_shape=pltpu.VMEM((count, width), jnp.float32),
        compiler_params=pltpu.CompilerParams(vmem_limit_bytes=32 << 20),
        cost_estimate=pl.CostEstimate(
            flops=4 * count * width * width,
            bytes_accessed=8 * count * width,
            transcendentals=count * width,
        ),
        name="slot_gate",
    )(cust_count, hc_edge, hp_edge, w_cust, w_prod)


def terms_kernel(half_ref, at_ref, hc_ref, hp_ref, delta_ref, out_ref):
    delta = delta_ref[...]
    columns = hc_ref.shape[1]
    products = out_ref.shape[0] - 2 * columns
    wanted = half_ref[0] * products + lax.broadcasted_iota(jnp.int32, (products, 1), 0)
    hot = jnp.where(at_ref[...] == wanted, jnp.bfloat16(1), jnp.bfloat16(0))
    contract = (((0,), (0,)), ((), ()))
    parts = (
        jnp.dot(hot, delta, preferred_element_type=jnp.float32),
        lax.dot_general(hc_ref[...], delta, contract, preferred_element_type=jnp.float32),
        lax.dot_general(hp_ref[...], delta, contract, preferred_element_type=jnp.float32),
    )
    starts = (0, products, products + columns)

    @pl.when(pl.program_id(0) == 0)
    def _():
        for at, part in zip(starts, parts):
            out_ref[at : at + part.shape[0], :] = part

    @pl.when(pl.program_id(0) > 0)
    def _():
        for at, part in zip(starts, parts):
            out_ref[at : at + part.shape[0], :] += part


def half_terms(half, prod_at, hc_edge, hp_edge, delta, products, tile=2048):
    count, width = delta.shape
    tile = min(tile, count)
    columns = width // 2
    rows = products // 2 + 2 * columns
    edge = pl.BlockSpec((tile, columns), lambda i, h: (i, h[0]))
    return pl.pallas_call(
        terms_kernel,
        grid_spec=pltpu.PrefetchScalarGridSpec(
            num_scalar_prefetch=1,
            grid=(count // tile,),
            in_specs=[
                pl.BlockSpec((1, tile), lambda i, h: (0, i)),
                edge,
                edge,
                pl.BlockSpec((tile, width), lambda i, h: (i, 0)),
            ],
            out_specs=pl.BlockSpec((rows, width), lambda i, h: (0, 0)),
        ),
        out_shape=jax.ShapeDtypeStruct((rows, width), jnp.float32),
        compiler_params=pltpu.CompilerParams(vmem_limit_bytes=32 << 20),
        cost_estimate=pl.CostEstimate(
            flops=2 * count * rows * width, bytes_accessed=4 * count * width, transcendentals=0
        ),
        name="half_terms",
    )(half.reshape(1), prod_at.reshape(1, count), hc_edge, hp_edge, delta)


def owner_sum_kernel(key_ref, rows_ref, *refs):
    out_ref = refs[-1]
    tile = out_ref.shape[0]
    wanted = pl.program_id(0) * tile + lax.broadcasted_iota(jnp.int32, (tile, 1), 0)
    hot = jnp.where(key_ref[...] == wanted, jnp.bfloat16(1), jnp.bfloat16(0))
    out_ref[...] = jnp.dot(hot, rows_ref[...], preferred_element_type=jnp.float32)


def owner_sum(keys, rows, owned, width, at, earlier=None, tile=1024):
    count, columns = rows.shape
    tile = min(tile, owned)
    in_specs = [
        pl.BlockSpec((1, count), lambda i: (0, 0)),
        pl.BlockSpec((count, columns), lambda i: (0, 0)),
    ]
    operands = [keys.reshape(1, count), rows]
    aliases = {}
    if earlier is not None:
        in_specs.append(pl.BlockSpec(memory_space=pl.ANY))
        operands.append(earlier)
        aliases = {2: 0}
    return pl.pallas_call(
        owner_sum_kernel,
        grid=(owned // tile,),
        out_shape=jax.ShapeDtypeStruct((owned, width), jnp.float32),
        in_specs=in_specs,
        out_specs=pl.BlockSpec((tile, columns), lambda i: (i, at // columns)),
        input_output_aliases=aliases,
        compiler_params=pltpu.CompilerParams(vmem_limit_bytes=32 << 20),
        cost_estimate=pl.CostEstimate(
            flops=0 if earlier is None else 2 * owned * columns * count,
            bytes_accessed=0 if earlier is None else 2 * count * columns + 4 * owned * columns,
            transcendentals=0,
        ),
        name="owner_sum",
    )(*operands)


def delta_kernel(keep, at, got_ref, product_ref, gate_ref, weight_ref, *out_refs):
    upstream = got_ref[...].astype(jnp.float32) + product_ref[...].astype(jnp.float32)
    delta = (upstream * gate_ref[...]).astype(jnp.bfloat16)
    if keep:
        out_refs[1][...] = delta
    out_ref = out_refs[0]
    part = weight_ref[at : at + out_ref.shape[1], :]
    out_ref[...] = lax.dot_general(
        delta, part, (((1,), (1,)), ((), ())), preferred_element_type=jnp.float32
    ).astype(jnp.bfloat16)


def delta_and_rows(got, product_rows, gate, weight, at, columns, keep, tile=1024):
    count, width = got.shape
    tile = min(tile, count)
    slots = lambda wide: pl.BlockSpec((tile, wide), lambda i: (i, 0))
    return pl.pallas_call(
        functools.partial(delta_kernel, keep, at),
        grid=(count // tile,),
        in_specs=[
            slots(width),
            slots(width),
            slots(width),
            pl.BlockSpec((width, width), lambda i: (0, 0)),
        ],
        out_specs=[slots(columns)] + [slots(width)] * keep,
        out_shape=[pltpu.HBM((count, columns), jnp.bfloat16)]
        + [jax.ShapeDtypeStruct((count, width), jnp.bfloat16)] * keep,
        compiler_params=pltpu.CompilerParams(vmem_limit_bytes=56 << 20),
        cost_estimate=pl.CostEstimate(
            flops=2 * count * width * width, bytes_accessed=12 * count * width, transcendentals=0
        ),
        name="delta_and_rows",
    )(got, product_rows, gate, weight)


def place():
    row = lax.axis_index("rows")
    return row % 2, row // 2, lax.axis_index("grp")


def spread(mine, shift, size, step, here):
    blocks = [mine] + [shift(mine, step * k) for k in range(1, size)]
    stacked = jnp.zeros((size,) + mine.shape, mine.dtype)
    for k, block in enumerate(blocks):
        stacked = lax.dynamic_update_index_in_dim(stacked, block, here ^ k, 0)
    return stacked


def gather_grp(mine):
    return spread(mine, shift_grp, lax.axis_size("grp"), 1, lax.axis_index("grp"))


def gather_rows(own):
    core, plane, grp = place()
    own = spread(own, shift_rows, lax.axis_size("rows") // 2, 2, plane)
    other = shift_rows(own, 1)
    first = core == 0
    return jnp.stack([jnp.where(first, own, other), jnp.where(first, other, own)])


def fold(terms, shift, size, step, here):
    total = lax.dynamic_index_in_dim(terms, here, 0, False)
    leaving = terms.astype(jnp.bfloat16)
    for k in range(1, size):
        sent = lax.dynamic_index_in_dim(leaving, here ^ k, 0, False)
        total = total + shift(sent, step * k).astype(jnp.float32)
    return total


def body(hc_edge, hp_edge, cust_count, recv_key, prod_key, cust_grad, prod_grad, w_cust, w_prod):
    devices = lax.axis_size(AXES)
    grps = lax.axis_size("grp")
    planes = lax.axis_size("rows") // 2
    slot_count, width = hc_edge.shape
    capacity = slot_count // devices
    product_count = prod_grad.shape[0]
    grid = (2, planes, grps)

    products = gather_grp(prod_grad)
    owned_rows = pick(cust_grad, recv_key, pltpu.HBM, 60)
    owned_rows, products = lax.optimization_barrier((owned_rows, products))
    fetched = lax.all_to_all(
        owned_rows.reshape(devices, capacity, width), AXES, split_axis=0, concat_axis=0, tiled=True
    ).reshape(slot_count, width)

    owner, low = prod_key // product_count, prod_key % product_count
    row, grp = owner // grps, owner % grps
    prod_at = (((row % 2) * planes + row // 2) * grps + grp) * product_count + low
    product_table = gather_rows(products).reshape(devices * product_count, width)
    product_rows = pick(product_table, prod_at, jax.ShapeDtypeStruct, 16)

    gate = slot_gate(cust_count, hc_edge, hp_edge, w_cust, w_prod)
    cut = width * 3 // 4
    parts = (fetched, product_rows, gate, w_cust)
    (first,) = delta_and_rows(*parts, 0, cut, False)
    second, delta = delta_and_rows(*parts, cut, width - cut, True)

    def give_back(rows):
        return lax.all_to_all(
            rows.reshape(devices, capacity, -1), AXES, split_axis=0, concat_axis=0, tiled=True
        ).reshape(slot_count, -1)

    returned = give_back(first)

    core, plane, _ = place()
    products = devices * product_count
    sent = half_terms(1 - core, prod_at, hc_edge, hp_edge, delta, products)
    kept = half_terms(core, prod_at, hc_edge, hp_edge, delta, products)
    kept = kept + shift_rows(sent, 1)
    cuts = (0, products // 2, products // 2 + width // 2, products // 2 + width)
    terms = jnp.concatenate(
        [kept[a:b].reshape(planes, grps, -1, width) for a, b in zip(cuts, cuts[1:])], axis=2
    )
    leaving = terms.astype(jnp.bfloat16)
    got = [
        shift_rows(lax.dynamic_index_in_dim(leaving, plane ^ k, 0, False), 2 * k)
        for k in range(1, planes)
    ]
    mine = lax.dynamic_index_in_dim(terms, plane, 0, False)
    for block in got:
        mine = mine + block.astype(jnp.float32)
    here = lax.axis_index("grp")
    weights = mine[:, product_count:]
    asked = [
        lax.dynamic_index_in_dim(mine[:, :product_count], here ^ k, 0, False) for k in range(grps)
    ]
    step = 1
    while step < grps:
        kept, sent = asked[0 :: 2 * step], asked[step :: 2 * step]
        packed = jnp.concatenate(sent + [weights.reshape(-1, width)])
        if 2 * step >= grps:
            packed = packed.astype(jnp.bfloat16)
            weights = weights.astype(jnp.bfloat16).astype(jnp.float32)
        packed = shift_grp(packed, step)
        if step == 1:
            packed, returned, second = lax.optimization_barrier((packed, returned, second))
        block = packed.astype(jnp.float32)
        for k in range(len(kept)):
            asked[2 * step * k] = kept[k] + block[k * product_count : (k + 1) * product_count]
        weights = weights + block[len(kept) * product_count :].reshape(weights.shape)
        step *= 2
    own_sum = asked[0]
    own = weights.astype(jnp.bfloat16)
    own, own_sum, returned = lax.optimization_barrier((own, own_sum, returned))
    returned_second = give_back(second)
    grad_scale = 1.0 / math.sqrt(slot_count * devices)
    share = width // devices
    owned = cust_grad.shape[0]
    high = own_sum.astype(jnp.bfloat16)
    low_part = (own_sum - high.astype(jnp.float32)).astype(jnp.bfloat16)
    both_parts = lax.dot_general(
        jnp.concatenate([high, low_part]),
        w_prod,
        (((1,), (1,)), ((), ())),
        preferred_element_type=jnp.float32,
    )
    prod_table_grad = (both_parts[:product_count] + both_parts[product_count:]) * math.sqrt(
        product_count / slot_count
    )
    table = owner_sum(recv_key, returned, owned, width, 0)
    own = spread(own, shift_rows, planes, 2, plane)
    own, table, prod_table_grad = lax.optimization_barrier((own, table, prod_table_grad))
    other = shift_rows(own, 1)
    cust_table_grad = owner_sum(recv_key, returned_second, owned, width, cut, table)
    other, cust_table_grad = lax.optimization_barrier((other, cust_table_grad))

    def whole(share_at):
        pick_share = slice(share_at, share_at + share)
        mine_part, other_part = own[:, :, pick_share], other[:, :, pick_share]
        first = lax.axis_index("rows") % 2 == 0
        both = [jnp.where(first, mine_part, other_part), jnp.where(first, other_part, mine_part)]
        return jnp.stack(both).astype(jnp.float32).reshape(width, width) * grad_scale

    return cust_table_grad, prod_table_grad, whole(0), whole(share)


def solution(mesh):
    rows = P(AXES, None)
    placed = (rows, rows, rows, P(AXES), P(AXES), rows, rows, P(), P())
    return jax.shard_map(
        body,
        mesh=mesh,
        in_specs=placed,
        out_specs=(rows, rows, P(), P()),
        check_vma=False,
    )
```

```python
import functools
import math

import jax
import jax.numpy as jnp
from jax import lax
from jax.experimental import pallas as pl
from jax.experimental.pallas import tpu as pltpu
from jax.sharding import PartitionSpec as P

AXES = ("rows", "grp")


def shift_rows(value, mask):
    size = lax.axis_size("rows")
    return lax.ppermute(value, "rows", [(i, i ^ mask) for i in range(size)])


def shift_grp(value, mask):
    size = lax.axis_size("grp")
    return lax.ppermute(value, "grp", [(i, i ^ mask) for i in range(size)])


def pick_kernel(key_ref, table_ref, out_ref):
    tile, length = key_ref.shape[1], table_ref.shape[0]
    keys = jnp.transpose(jnp.broadcast_to(key_ref[...], (128, tile)))
    lane = lax.broadcasted_iota(jnp.int32, (tile, 128), 1)
    one, zero = jnp.bfloat16(1), jnp.bfloat16(0)
    hot = jnp.concatenate(
        [jnp.where(keys == lane + at, one, zero) for at in range(0, length, 128)], axis=1
    )
    out_ref[...] = jnp.dot(hot, table_ref[...], preferred_element_type=jnp.float32).astype(
        jnp.bfloat16
    )


def pick(table, keys, space, limit, tile=1024):
    length, width = table.shape
    count = keys.shape[0]
    tile = min(tile, count)
    return pl.pallas_call(
        pick_kernel,
        grid=(count // tile,),
        out_shape=space((count, width), jnp.bfloat16),
        in_specs=[
            pl.BlockSpec((1, tile), lambda i: (0, i)),
            pl.BlockSpec((length, width), lambda i: (0, 0)),
        ],
        out_specs=pl.BlockSpec((tile, width), lambda i: (i, 0)),
        compiler_params=pltpu.CompilerParams(vmem_limit_bytes=limit << 20),
        cost_estimate=pl.CostEstimate(
            flops=2 * count * length * width,
            bytes_accessed=2 * (length + count) * width,
            transcendentals=0,
        ),
        name="pick_rows",
    )(keys.reshape(1, count), table)


def gate_kernel(count_ref, hc_ref, hp_ref, wc_ref, wp_ref, out_ref, *, capacity):
    blocks = out_ref.shape[0] // capacity
    preact = jnp.dot(hc_ref[...], wc_ref[...], preferred_element_type=jnp.float32) + jnp.dot(
        hp_ref[...], wp_ref[...], preferred_element_type=jnp.float32
    )
    squashed = jax.nn.sigmoid(preact)
    slot = lax.broadcasted_iota(jnp.int32, (capacity, 1), 0)
    first = pl.program_id(0) * blocks
    live = jnp.concatenate([slot < count_ref[0, first + k] for k in range(blocks)])
    out_ref[...] = jnp.where(live, squashed * (1.0 + preact * (1.0 - squashed)), 0.0)


def slot_gate(cust_count, hc_edge, hp_edge, w_cust, w_prod, tile=512):
    count, width = hc_edge.shape
    tile = min(tile, count)
    slots = pl.BlockSpec((tile, width), lambda i, c: (i, 0))
    whole = pl.BlockSpec((width, width), lambda i, c: (0, 0))
    return pl.pallas_call(
        functools.partial(gate_kernel, capacity=count // cust_count.shape[1]),
        grid_spec=pltpu.PrefetchScalarGridSpec(
            num_scalar_prefetch=1,
            grid=(count // tile,),
            in_specs=[slots, slots, whole, whole],
            out_specs=slots,
        ),
        out_shape=pltpu.VMEM((count, width), jnp.float32),
        compiler_params=pltpu.CompilerParams(vmem_limit_bytes=32 << 20),
        cost_estimate=pl.CostEstimate(
            flops=4 * count * width * width,
            bytes_accessed=8 * count * width,
            transcendentals=count * width,
        ),
        name="slot_gate",
    )(cust_count, hc_edge, hp_edge, w_cust, w_prod)


def terms_kernel(half_ref, at_ref, hc_ref, hp_ref, delta_ref, out_ref):
    delta = delta_ref[...]
    columns = hc_ref.shape[1]
    products = out_ref.shape[0] - 2 * columns
    wanted = half_ref[0] * products + lax.broadcasted_iota(jnp.int32, (products, 1), 0)
    hot = jnp.where(at_ref[...] == wanted, jnp.bfloat16(1), jnp.bfloat16(0))
    contract = (((0,), (0,)), ((), ()))
    parts = (
        jnp.dot(hot, delta, preferred_element_type=jnp.float32),
        lax.dot_general(hc_ref[...], delta, contract, preferred_element_type=jnp.float32),
        lax.dot_general(hp_ref[...], delta, contract, preferred_element_type=jnp.float32),
    )
    starts = (0, products, products + columns)

    @pl.when(pl.program_id(0) == 0)
    def _():
        for at, part in zip(starts, parts):
            out_ref[at : at + part.shape[0], :] = part

    @pl.when(pl.program_id(0) > 0)
    def _():
        for at, part in zip(starts, parts):
            out_ref[at : at + part.shape[0], :] += part


def half_terms(half, prod_at, hc_edge, hp_edge, delta, products, tile=2048):
    count, width = delta.shape
    tile = min(tile, count)
    columns = width // 2
    rows = products // 2 + 2 * columns
    edge = pl.BlockSpec((tile, columns), lambda i, h: (i, h[0]))
    return pl.pallas_call(
        terms_kernel,
        grid_spec=pltpu.PrefetchScalarGridSpec(
            num_scalar_prefetch=1,
            grid=(count // tile,),
            in_specs=[
                pl.BlockSpec((1, tile), lambda i, h: (0, i)),
                edge,
                edge,
                pl.BlockSpec((tile, width), lambda i, h: (i, 0)),
            ],
            out_specs=pl.BlockSpec((rows, width), lambda i, h: (0, 0)),
        ),
        out_shape=jax.ShapeDtypeStruct((rows, width), jnp.float32),
        compiler_params=pltpu.CompilerParams(vmem_limit_bytes=32 << 20),
        cost_estimate=pl.CostEstimate(
            flops=2 * count * rows * width, bytes_accessed=4 * count * width, transcendentals=0
        ),
        name="half_terms",
    )(half.reshape(1), prod_at.reshape(1, count), hc_edge, hp_edge, delta)


def owner_sum_kernel(key_ref, rows_ref, *refs):
    out_ref = refs[-1]
    tile = out_ref.shape[0]
    wanted = pl.program_id(0) * tile + lax.broadcasted_iota(jnp.int32, (tile, 1), 0)
    hot = jnp.where(key_ref[...] == wanted, jnp.bfloat16(1), jnp.bfloat16(0))
    out_ref[...] = jnp.dot(hot, rows_ref[...], preferred_element_type=jnp.float32)


def owner_sum(keys, rows, owned, width, at, earlier=None, tile=1024):
    count, columns = rows.shape
    tile = min(tile, owned)
    in_specs = [
        pl.BlockSpec((1, count), lambda i: (0, 0)),
        pl.BlockSpec((count, columns), lambda i: (0, 0)),
    ]
    operands = [keys.reshape(1, count), rows]
    aliases = {}
    if earlier is not None:
        in_specs.append(pl.BlockSpec(memory_space=pl.ANY))
        operands.append(earlier)
        aliases = {2: 0}
    return pl.pallas_call(
        owner_sum_kernel,
        grid=(owned // tile,),
        out_shape=jax.ShapeDtypeStruct((owned, width), jnp.float32),
        in_specs=in_specs,
        out_specs=pl.BlockSpec((tile, columns), lambda i: (i, at // columns)),
        input_output_aliases=aliases,
        compiler_params=pltpu.CompilerParams(vmem_limit_bytes=32 << 20),
        cost_estimate=pl.CostEstimate(
            flops=0 if earlier is None else 2 * owned * columns * count,
            bytes_accessed=0 if earlier is None else 2 * count * columns + 4 * owned * columns,
            transcendentals=0,
        ),
        name="owner_sum",
    )(*operands)


def delta_kernel(keep, at, got_ref, product_ref, gate_ref, weight_ref, *out_refs):
    upstream = got_ref[...].astype(jnp.float32) + product_ref[...].astype(jnp.float32)
    delta = (upstream * gate_ref[...]).astype(jnp.bfloat16)
    if keep:
        out_refs[1][...] = delta
    out_ref = out_refs[0]
    part = weight_ref[at : at + out_ref.shape[1], :]
    out_ref[...] = lax.dot_general(
        delta, part, (((1,), (1,)), ((), ())), preferred_element_type=jnp.float32
    ).astype(jnp.bfloat16)


def delta_and_rows(got, product_rows, gate, weight, at, columns, keep, tile=1024):
    count, width = got.shape
    tile = min(tile, count)
    slots = lambda wide: pl.BlockSpec((tile, wide), lambda i: (i, 0))
    return pl.pallas_call(
        functools.partial(delta_kernel, keep, at),
        grid=(count // tile,),
        in_specs=[
            slots(width),
            slots(width),
            slots(width),
            pl.BlockSpec((width, width), lambda i: (0, 0)),
        ],
        out_specs=[slots(columns)] + [slots(width)] * keep,
        out_shape=[pltpu.HBM((count, columns), jnp.bfloat16)]
        + [jax.ShapeDtypeStruct((count, width), jnp.bfloat16)] * keep,
        compiler_params=pltpu.CompilerParams(vmem_limit_bytes=56 << 20),
        cost_estimate=pl.CostEstimate(
            flops=2 * count * width * width, bytes_accessed=12 * count * width, transcendentals=0
        ),
        name="delta_and_rows",
    )(got, product_rows, gate, weight)


def place():
    row = lax.axis_index("rows")
    return row % 2, row // 2, lax.axis_index("grp")


def spread(mine, shift, size, step, here):
    blocks = [mine] + [shift(mine, step * k) for k in range(1, size)]
    stacked = jnp.zeros((size,) + mine.shape, mine.dtype)
    for k, block in enumerate(blocks):
        stacked = lax.dynamic_update_index_in_dim(stacked, block, here ^ k, 0)
    return stacked


def gather_grp(mine):
    return spread(mine, shift_grp, lax.axis_size("grp"), 1, lax.axis_index("grp"))


def gather_rows(own):
    core, plane, grp = place()
    own = spread(own, shift_rows, lax.axis_size("rows") // 2, 2, plane)
    other = shift_rows(own, 1)
    first = core == 0
    return jnp.stack([jnp.where(first, own, other), jnp.where(first, other, own)])


def fold(terms, shift, size, step, here):
    total = lax.dynamic_index_in_dim(terms, here, 0, False)
    leaving = terms.astype(jnp.bfloat16)
    for k in range(1, size):
        sent = lax.dynamic_index_in_dim(leaving, here ^ k, 0, False)
        total = total + shift(sent, step * k).astype(jnp.float32)
    return total


def body(hc_edge, hp_edge, cust_count, recv_key, prod_key, cust_grad, prod_grad, w_cust, w_prod):
    devices = lax.axis_size(AXES)
    grps = lax.axis_size("grp")
    planes = lax.axis_size("rows") // 2
    slot_count, width = hc_edge.shape
    capacity = slot_count // devices
    product_count = prod_grad.shape[0]
    grid = (2, planes, grps)

    products = gather_grp(prod_grad)
    owned_rows = pick(cust_grad, recv_key, pltpu.HBM, 60)
    owned_rows, products = lax.optimization_barrier((owned_rows, products))
    fetched = lax.all_to_all(
        owned_rows.reshape(devices, capacity, width), AXES, split_axis=0, concat_axis=0, tiled=True
    ).reshape(slot_count, width)

    owner, low = prod_key // product_count, prod_key % product_count
    row, grp = owner // grps, owner % grps
    prod_at = (((row % 2) * planes + row // 2) * grps + grp) * product_count + low
    product_table = gather_rows(products).reshape(devices * product_count, width)
    product_rows = pick(product_table, prod_at, jax.ShapeDtypeStruct, 16)

    gate = slot_gate(cust_count, hc_edge, hp_edge, w_cust, w_prod)
    cut = width * 3 // 4
    parts = (fetched, product_rows, gate, w_cust)
    (first,) = delta_and_rows(*parts, 0, cut, False)
    second, delta = delta_and_rows(*parts, cut, width - cut, True)

    def give_back(rows):
        return lax.all_to_all(
            rows.reshape(devices, capacity, -1), AXES, split_axis=0, concat_axis=0, tiled=True
        ).reshape(slot_count, -1)

    returned = give_back(first)

    core, plane, _ = place()
    products = devices * product_count
    sent = half_terms(1 - core, prod_at, hc_edge, hp_edge, delta, products)
    kept = half_terms(core, prod_at, hc_edge, hp_edge, delta, products)
    kept = kept + shift_rows(sent, 1)
    cuts = (0, products // 2, products // 2 + width // 2, products // 2 + width)
    terms = jnp.concatenate(
        [kept[a:b].reshape(planes, grps, -1, width) for a, b in zip(cuts, cuts[1:])], axis=2
    )
    leaving = terms.astype(jnp.bfloat16)
    got = [
        shift_rows(lax.dynamic_index_in_dim(leaving, plane ^ k, 0, False), 2 * k)
        for k in range(1, planes)
    ]
    mine = lax.dynamic_index_in_dim(terms, plane, 0, False)
    for block in got:
        mine = mine + block.astype(jnp.float32)
    here = lax.axis_index("grp")
    sums, weights = mine[:, :product_count], mine[:, product_count:].astype(jnp.bfloat16)
    every = weights.reshape(-1, width)
    own_sum = lax.dynamic_index_in_dim(sums, here, 0, False)
    blocks = [
        shift_grp(
            jnp.concatenate(
                [lax.dynamic_index_in_dim(sums, here ^ k, 0, False).astype(jnp.bfloat16), every]
            ),
            k,
        )
        for k in range(1, grps)
    ]
    blocks, returned = lax.optimization_barrier((blocks, returned))
    terms = [weights.astype(jnp.float32)]
    for block in blocks:
        own_sum = own_sum + block[:product_count].astype(jnp.float32)
        terms.append(block[product_count:].astype(jnp.float32).reshape(weights.shape))
    while len(terms) > 1:
        terms = [a + b for a, b in zip(terms[::2], terms[1::2])]
    own = terms[0].astype(jnp.bfloat16)
    returned_second = give_back(second)
    grad_scale = 1.0 / math.sqrt(slot_count * devices)
    share = width // devices
    owned = cust_grad.shape[0]
    high = own_sum.astype(jnp.bfloat16)
    low_part = (own_sum - high.astype(jnp.float32)).astype(jnp.bfloat16)
    both_parts = lax.dot_general(
        jnp.concatenate([high, low_part]),
        w_prod,
        (((1,), (1,)), ((), ())),
        preferred_element_type=jnp.float32,
    )
    prod_table_grad = (both_parts[:product_count] + both_parts[product_count:]) * math.sqrt(
        product_count / slot_count
    )
    table = owner_sum(recv_key, returned, owned, width, 0)
    own = spread(own, shift_rows, planes, 2, plane)
    own, table, prod_table_grad = lax.optimization_barrier((own, table, prod_table_grad))
    other = shift_rows(own, 1)
    cust_table_grad = owner_sum(recv_key, returned_second, owned, width, cut, table)
    other, cust_table_grad = lax.optimization_barrier((other, cust_table_grad))

    def whole(share_at):
        pick_share = slice(share_at, share_at + share)
        mine_part, other_part = own[:, :, pick_share], other[:, :, pick_share]
        first = lax.axis_index("rows") % 2 == 0
        both = [jnp.where(first, mine_part, other_part), jnp.where(first, other_part, mine_part)]
        return jnp.stack(both).astype(jnp.float32).reshape(width, width) * grad_scale

    return cust_table_grad, prod_table_grad, whole(0), whole(share)


def solution(mesh):
    rows = P(AXES, None)
    placed = (rows, rows, rows, P(AXES), P(AXES), rows, rows, P(), P())
    return jax.shard_map(
        body,
        mesh=mesh,
        in_specs=placed,
        out_specs=(rows, rows, P(), P()),
        check_vma=False,
    )
```
